128 devices in a mesh: lon: 32 (over z, x, core), lat: 4 (over y).
Axes of the slice: x: 4, y: 4, z: 4, core: 2. Of those that a mesh axis runs over, the one named last changes fastest.
Arguments:
- guide: float32 [512, 32768], P('lat', 'lon'), may hold values from -8 to 8
- screen: float32 [512, 32768], P('lat', 'lon'), may hold values from 0.001 to 0.1
- valid: int32 [512, 32768], P('lat', 'lon'), may hold values 0 or 1
- tiles: int32 [4, 256], P('lat', 'lon'), may hold values 0 or 1
Outputs:
- solution_field: float32 [512, 32768], P('lat', 'lon')
- residual: float32 [512, 32768], P('lat', 'lon')
The draws below stay inside these ranges and needn't reach their ends.
All inputs are finite; a program needn't handle non-finite values. No bound on the sum of `valid` or of `tiles` on one device may be relied on, other than what follows from the above.
Results may differ from the reference program's by a relative error of at most 0.00012.
Values sent between devices are 32-bit elements; how exact they have to be, the bound alone decides.
A program may use at most 128 MiB of HBM per device.

```python
import math
import jax
import jax.numpy as jnp

TILE = 128
LEVELS = 4
SMOOTH = 2
COARSE_SWEEPS = 8
CYCLES = 2
NLAT = 512
NLON = 32768


def plant(entries, key, smallest, high):
    longest = entries.shape.index(max(entries.shape))
    spots = []
    for shift in (0, 1):
        where = [jax.random.randint(jax.random.fold_in(key, axis), (), 0, length) for axis, length in enumerate(entries.shape)]
        where[longest] = (where[longest] + shift) % entries.shape[longest]
        spots.append(tuple(where))
    return entries.at[spots[0]].set(smallest).at[spots[1]].set(high)


def level_of(key, extent, split, smallest, top_value):
    level = 1.0
    for dim, blocks in split:
        steps = jax.random.uniform(jax.random.fold_in(jax.random.fold_in(key, 6), dim), (blocks,), jnp.float32, smallest / len(split), top_value / len(split))
        level = level * jnp.repeat(jnp.exp(steps), extent[dim] // blocks).reshape((-1,) + (1,) * (len(extent) - 1 - dim))
    return level


def noise(stream_key, shape, deviation, most, shards=(), held_as=jnp.bfloat16):
    entries = jax.random.normal(stream_key, shape, jnp.float32) * deviation
    if len(shards) > 0:
        entries = level_of(stream_key, shape, shards, -0.22, 0.18) * entries
    return jnp.clip(entries, min=-most, max=most).astype(held_as)


def setup_inputs(seed: int = 0) -> dict:
    splits = jax.random.split(jax.random.key(seed), 5)
    guide = noise(splits[0], (NLAT, NLON), 1.0, 8.0, ((0, 4), (1, 32)), jnp.float32)
    screen = jnp.clip(jnp.exp(math.log(0.1) - 4.6051702 * jax.random.uniform(splits[1], (NLAT, NLON), jnp.float32) ** level_of(splits[1], (NLAT, NLON), ((0, 4), (1, 32)), -0.2, 0.2)), 0.001, 0.1)
    valid = plant((jax.random.randint(splits[2], (NLAT, NLON), 0, 8) < 7).astype(jnp.int32), jax.random.fold_in(splits[2], 1), 0, 1)
    tiles = plant((jax.random.randint(splits[3], (NLAT // TILE, NLON // TILE), 0, 4) < 3).astype(jnp.int32), jax.random.fold_in(splits[3], 1), 0, 1)
    return {"guide": guide, "screen": screen, "valid": valid, "tiles": tiles}


OMEGA = 0.8


def stencil(field, weight):
    padded = jnp.pad(field, ((1, 1), (0, 0)))
    upper = padded[:-2]
    lower = padded[2:]
    left = jnp.roll(field, 1, 1)
    right = jnp.roll(field, -1, 1)
    return (4.0 + weight) * field - (((upper + lower) + left) + right)


def relax(field, source, weight, active):
    return field + OMEGA * active * (source - stencil(field, weight)) / (4.0 + weight)


def block_sum(field):
    rows, cols = field.shape
    return field.reshape(rows // 2, 2, cols // 2, 2).sum(axis=(1, 3))


def block_max(field):
    rows, cols = field.shape
    return field.reshape(rows // 2, 2, cols // 2, 2).max(axis=(1, 3))


def expand(field):
    return jnp.repeat(jnp.repeat(field, 2, 0), 2, 1)


def vcycle(level, source, weights, actives):
    field = jnp.zeros_like(source)
    if level == LEVELS - 1:
        for sweep in range(COARSE_SWEEPS):
            field = relax(field, source, weights[level], actives[level])
        return field
    for sweep in range(SMOOTH):
        field = relax(field, source, weights[level], actives[level])
    resid = actives[level] * (source - stencil(field, weights[level]))
    coarse_src = actives[level + 1] * block_sum(resid)
    correction = vcycle(level + 1, coarse_src, weights, actives)
    field = field + actives[level] * expand(correction)
    for sweep in range(SMOOTH):
        field = relax(field, source, weights[level], actives[level])
    return field


def reference(guide, screen, valid, tiles):
    flags = jnp.repeat(jnp.repeat(tiles.astype(jnp.float32), TILE, 0), TILE, 1)
    active = valid.astype(jnp.float32) * flags
    weights = [screen]
    actives = [active]
    for level in range(LEVELS - 1):
        weights.append(block_sum(weights[-1]))
        actives.append(block_max(actives[-1]))
    source = active * guide
    solution_field = jnp.zeros_like(guide)
    for cycle in range(CYCLES):
        resid = active * (source - stencil(solution_field, screen))
        solution_field = solution_field + vcycle(0, resid, weights, actives)
    residual = active * (source - stencil(solution_field, screen))
    return solution_field, residual
```

```python
import functools

import jax
import jax.numpy as jnp
from jax import lax
from jax.experimental import pallas as pl
from jax.experimental.pallas import tpu as pltpu
from jax.sharding import PartitionSpec as P

OMEGA = 0.8
MESH = pl.DeviceIdType.MESH
LANES = 128

T0, O0, N0 = 9, 24, 128
T1, O1, N1 = 5, 16, 64
T2, O2, N2 = 3, 32, 32
T3, O3, N3 = 2, 20, 16
R0, R1, R2, R3 = 176, 96, 96, 56
A0, A1, A2, A3 = (8, 168), (8, 88), (8, 88), (8, 48)
H0, H1, H2 = 16, 8, 24
DIRS = ((-1, 0), (1, 0), (0, -1), (0, 1), (-1, -1), (-1, 1), (1, -1), (1, 1))


def lanes_of(x):
    return lax.broadcasted_iota(jnp.int32, x.shape, 1)


def neighbours(src, t, count, lo, hi):
    x = src[t, lo:hi]
    lane = lanes_of(x)
    left = pltpu.roll(jnp.where(lane == LANES - 1, src[(t - 1) % count, lo:hi], x), 1, 1)
    right = pltpu.roll(jnp.where(lane == 0, src[(t + 1) % count, lo:hi], x), LANES - 1, 1)
    return x, ((src[t, lo - 1:hi - 1] + src[t, lo + 1:hi + 1]) + left) + right


def sweep(src, dst, g, b, count, lo, hi):
    for t in range(count):
        x, near = neighbours(src, t, count, lo, hi)
        dst[t, lo:hi] = (1.0 - OMEGA) * x + b[t, lo:hi] * (g[t, lo:hi] + near)


def first_sweep(dst, g, b, count, lo, hi):
    for t in range(count):
        dst[t, lo:hi] = b[t, lo:hi] * g[t, lo:hi]


def residual_of(src, dst, g, e, count, lo, hi, tiles):
    for t in range(tiles):
        x, near = neighbours(src, t, count, lo, hi)
        ee = e[t, lo:hi]
        dst[t, lo:hi] = jnp.where(ee > 0.0, (g[t, lo:hi] + near) - ee * x, 0.0)


def gather(x, index):
    return jnp.take_along_axis(x, index, axis=1, mode="promise_in_bounds")


def coarsen(src, t, tiles, lo, rows, op):
    def pair(tile):
        return op(src[tile, pl.ds(lo, rows, stride=2)], src[tile, pl.ds(lo + 1, rows, stride=2)])

    x = pair(2 * t)
    lane = lanes_of(x)
    x = op(x, pltpu.roll(x, LANES - 1, 1))
    if 2 * t + 1 < tiles:
        y = pair(2 * t + 1)
        x = jnp.where(lane % 2 == 0, x, op(y, pltpu.roll(y, 1, 1)))
        index = jnp.where(lane < LANES // 2, 2 * lane, 2 * lane - (LANES - 1))
    else:
        index = (2 * lane) % LANES
    return gather(x, index)


def correct(coarse, fine, e, count, clo, rows, lo):
    for t in range(count):
        c = coarse[t // 2, clo:clo + rows]
        lane = lanes_of(c)
        half = lane // 2
        if t == count - 1:
            index = jnp.where(lane < LANES // 2, half, LANES // 2 + half)
        else:
            index = half + (LANES // 2) * (t % 2)
        c = gather(c, index)
        for odd in range(2):
            rws = pl.ds(lo + odd, rows, stride=2)
            fine[t, rws] = fine[t, rws] + jnp.where(e[t, rws] > 0.0, c, 0.0)


def kernel(lon_count, lat_count, guide, screen, valid, tiles, out, res,
           gin, win, vin, fin, sb, e0, v0, w0, r0, vg, bb, e1, u1, r1, wa, b2, e2, gg, v2, u2, r2, b3, g3, v3, u3,
           xsb, xbb, xwa, xgg, xvg, rvg, in_sem, out_sem, send_sem, recv_sem):
    lon = lax.axis_index("lon")
    lat = lax.axis_index("lat")
    s0, b0 = sb.at[0], sb.at[1]
    v1, g1, b1 = vg.at[0], vg.at[1], bb.at[0]
    w2, a2 = wa.at[0], wa.at[1]

    loads = []
    for i, (src, dst) in enumerate(((screen, win), (valid, vin), (guide, gin))):
        for t in range(T0 - 1):
            loads.append(pltpu.make_async_copy(src.at[:, pl.ds(t * LANES, LANES)], dst.at[t], in_sem.at[i, t]))
    flag_copy = pltpu.make_async_copy(tiles, fin, in_sem.at[3, 0])
    flag_copy.start()
    for copy in loads:
        copy.start()

    def peer(d):
        return {"lat": lax.rem(lat + DIRS[d][0] + lat_count, lat_count), "lon": lax.rem(lon + DIRS[d][1] + lon_count, lon_count)}

    def exists(d):
        if DIRS[d][0] < 0:
            return lat > 0
        if DIRS[d][0] > 0:
            return lat < lat_count - 1
        return None

    def guarded(condition, fn):
        if condition is None:
            fn()
        else:
            pl.when(condition)(fn)

    barrier = pltpu.get_barrier_semaphore()
    for d in range(8):
        guarded(exists(d), lambda d=d: pl.semaphore_signal(
            barrier, inc=1, device_id=peer(d), device_id_type=MESH))

    for ref, rows, lo, hi in ((v0, R0, *A0), (w0, R0, *A0), (v1, R1, *A1), (u1, R1, *A1), (v2, R2, *A2),
                              (u2, R2, *A2), (v3, R3, *A3), (u3, R3, *A3)):
        zero = jnp.zeros((ref.shape[0], 8, LANES), jnp.float32)
        ref[:, lo - 8:lo] = zero
        ref[:, hi:hi + 8] = zero

    interior = jnp.logical_and(lat > 0, lat < lat_count - 1).astype(jnp.int32)
    pl.semaphore_wait(barrier, 5 + 3 * interior)

    def message(kind, d, src, rows_dst, land, count, first, rows, depth):
        dy, dx = DIRS[d]
        if dy < 0:
            from_rows, to_rows = pl.ds(first, depth), pl.ds(first + rows, depth)
        elif dy > 0:
            from_rows, to_rows = pl.ds(first + rows - depth, depth), pl.ds(first - depth, depth)
        else:
            from_rows = to_rows = pl.ds(first, rows)
        if dx == 0:
            src = src.at[:, pl.ds(0, count - 1), from_rows]
            dst = rows_dst.at[:, pl.ds(0, count - 1), to_rows]
        else:
            src = src.at[:, 0 if dx < 0 else count - 2, from_rows]
            dst = land.at[1 if dx < 0 else 0, :, to_rows]
        return pltpu.make_async_remote_copy(
            src_ref=src, dst_ref=dst, send_sem=send_sem.at[kind, d], recv_sem=recv_sem.at[kind, d],
            device_id=peer(d), device_id_type=MESH)

    def send(kind, *where):
        for d in range(8):
            guarded(exists(d), lambda d=d: message(kind, d, *where).start())

    def sent(kind, *where):
        for d in range(8):
            guarded(exists(d), lambda d=d: message(kind, d, *where).wait_send())

    def received(kind, *where):
        src, rows_dst, land, count, first, rows, depth = where
        for d in range(8):
            back = DIRS.index((-DIRS[d][0], -DIRS[d][1]))
            guarded(exists(back), lambda d=d: message(kind, d, *where).wait_recv())
        for outside, lo in ((lat == 0, first - depth), (lat == lat_count - 1, first + rows)):
            @pl.when(outside)
            def _():
                for k in range(rows_dst.shape[0]):
                    rows_dst[k, :, lo:lo + depth] = jnp.zeros((rows_dst.shape[1], depth, LANES), jnp.float32)
                    for side in range(2):
                        land[side, k, lo:lo + depth] = jnp.zeros((depth, LANES), jnp.float32)

    def merge(land, k, ref, count, lo, hi):
        left = land[0, k, lo:hi]
        ref[count - 1, lo:hi] = jnp.where(lanes_of(left) < LANES // 2, land[1, k, lo:hi], left)

    flag_copy.wait()
    for copy in loads:
        copy.wait()
    own = slice(O0, O0 + N0)
    for t in range(T0 - 1):
        active = vin[t].astype(jnp.float32) * fin[0, t].astype(jnp.float32)
        diag = 4.0 + win[t]
        s0[t, own] = active * gin[t]
        b0[t, own] = active * OMEGA / diag
        e0[t, own] = active * diag
        r0[t, own] = active
    msg0 = (0, sb, sb, xsb, T0, O0, N0, H0)
    send(*msg0)

    own1 = slice(O1, O1 + N1)
    for t in range(T1 - 1):
        active = coarsen(r0, t, T0 - 1, O0, N1, jnp.maximum)
        weight = coarsen(win, t, T0 - 1, 0, N1, jnp.add)
        diag = 4.0 + weight
        b1[t, own1] = active * OMEGA / diag
        e1[t, own1] = active * diag
        r1[t, own1] = active
        u1[t, own1] = weight
    msg1 = (1, bb, bb, xbb, T1, O1, N1, H1)
    send(*msg1)

    for t in range(T2 - 1):
        a2[t, O2:O2 + N2] = coarsen(r1, t, T1 - 1, O1, N2, jnp.maximum)
        w2[t, O2:O2 + N2] = coarsen(u1, t, T1 - 1, O1, N2, jnp.add)
    msg2 = (2, wa, wa, xwa, T2, O2, N2, H2)
    send(*msg2)

    def masked_inverse(x):
        return jnp.where(x > 0.0, OMEGA / jnp.where(x > 0.0, x, 1.0), 0.0)

    received(*msg0)
    for k in range(2):
        merge(xsb, k, sb.at[k], T0, *A0)
    for t in range(T0):
        for lo, hi in (A0,) if t == T0 - 1 else ((A0[0], O0), (O0 + N0, A0[1])):
            e0[t, lo:hi] = masked_inverse(b0[t, lo:hi])

    for cycle in range(2):
        g2 = gg.at[cycle, 0]
        if cycle == 0:
            first_sweep(w0, s0, b0, T0, *A0)
        else:
            sweep(v0, w0, s0, b0, T0, *A0)
        sweep(w0, v0, s0, b0, T0, *A0)
        residual_of(v0, r0, s0, e0, T0, *A0, T0)

        if cycle == 0:
            received(*msg1)
            merge(xbb, 0, b1, T1, *A1)
        for t in range(T1):
            g1[t, A1[0]:A1[1]] = jnp.where(
                b1[t, A1[0]:A1[1]] > 0.0, coarsen(r0, t, T0, A0[0], A1[1] - A1[0], jnp.add), 0.0)
        first_sweep(u1, g1, b1, T1, *A1)
        sweep(u1, v1, g1, b1, T1, *A1)
        residual_of(v1, r1, g1, e1, T1, O1, O1 + N1, T1 - 1)
        for t in range(T2 - 1):
            g2[t, O2:O2 + N2] = jnp.where(
                a2[t, O2:O2 + N2] > 0.0, coarsen(r1, t, T1 - 1, O1, N2, jnp.add), 0.0)
        msg_g = (3 + 2 * cycle, gg.at[cycle], gg.at[cycle], xgg.at[cycle], T2, O2, N2, H2)
        msg_v = (4 + 2 * cycle, vg, rvg.at[cycle], xvg.at[cycle], T1, O1, N1, H1)
        send(*msg_g)
        send(*msg_v)

        if cycle == 0:
            received(*msg2)
            for k in range(2):
                merge(xwa, k, wa.at[k], T2, *A2)
            for t in range(T2):
                lo, hi = A2
                diag = 4.0 + w2[t, lo:hi]
                b2[t, lo:hi] = a2[t, lo:hi] * OMEGA / diag
                e2[t, lo:hi] = a2[t, lo:hi] * diag
            for t in range(T3):
                lo, hi = A3
                b3[t, lo:hi] = coarsen(a2, t, T2, A2[0], hi - lo, jnp.maximum) * OMEGA / (
                    4.0 + coarsen(w2, t, T2, A2[0], hi - lo, jnp.add))
        received(*msg_g)
        merge(xgg.at[cycle], 0, g2, T2, *A2)
        first_sweep(u2, g2, b2, T2, *A2)
        sweep(u2, v2, g2, b2, T2, *A2)
        residual_of(v2, r2, g2, e2, T2, *A2, T2)
        for t in range(T3):
            lo, hi = A3
            g3[t, lo:hi] = jnp.where(b3[t, lo:hi] > 0.0, coarsen(r2, t, T2, A2[0], hi - lo, jnp.add), 0.0)
        first_sweep(v3, g3, b3, T3, *A3)
        for i in range(7):
            src, dst = (v3, u3) if i % 2 == 0 else (u3, v3)
            sweep(src, dst, g3, b3, T3, *A3)
        correct(u3, v2, e2, T2, A3[0], A3[1] - A3[0], A2[0])
        sweep(v2, u2, g2, b2, T2, *A2)
        sweep(u2, v2, g2, b2, T2, *A2)
        sent(*msg_g)

        sent(*msg_v)
        received(*msg_v)
        for k in range(2):
            for t in range(T1 - 1):
                for lo, hi in ((A1[0], O1), (O1 + N1, A1[1])):
                    vg[k, t, lo:hi] = rvg[cycle, k, t, lo:hi]
            merge(xvg.at[cycle], k, vg.at[k], T1, *A1)
        correct(v2, v1, b1, T1, O2 - 4, 40, A1[0])
        sweep(v1, u1, g1, b1, T1, *A1)
        sweep(u1, v1, g1, b1, T1, *A1)
        correct(v1, v0, e0, T0, A1[0], A1[1] - A1[0], A0[0])
        sweep(v0, w0, s0, b0, T0, *A0)
        sweep(w0, v0, s0, b0, T0, *A0)

    stores = []
    for i, (src, dst) in enumerate(((v0, out), (r0, res))):
        if i == 1:
            residual_of(v0, r0, s0, e0, T0, O0, O0 + N0, T0 - 1)
        for t in range(T0 - 1):
            stores.append(pltpu.make_async_copy(
                src.at[t, pl.ds(O0, N0)], dst.at[:, pl.ds(t * LANES, LANES)], out_sem.at[i, t]))
            stores[-1].start()
    sent(*msg0)
    sent(*msg1)
    sent(*msg2)
    for copy in stores:
        copy.wait()


def solution(mesh):
    def body(guide, screen, valid, tiles):
        def vmem(*shape):
            return pltpu.VMEM(shape + (LANES,), jnp.float32)

        block = jax.ShapeDtypeStruct(guide.shape, jnp.float32)
        return pl.pallas_call(
            functools.partial(kernel, mesh.shape["lon"], mesh.shape["lat"]),
            out_shape=(block, block),
            in_specs=[pl.BlockSpec(memory_space=pl.ANY)] * 4,
            out_specs=(pl.BlockSpec(memory_space=pl.ANY),) * 2,
            scratch_shapes=[
                vmem(T0 - 1, N0), vmem(T0 - 1, N0), pltpu.VMEM((T0 - 1, N0, LANES), jnp.int32),
                pltpu.SMEM((1, T0 - 1), jnp.int32),
                vmem(2, T0, R0), vmem(T0, R0), vmem(T0, R0), vmem(T0, R0), vmem(T0, R0),
                vmem(2, T1, R1), vmem(1, T1, R1), vmem(T1, R1), vmem(T1, R1), vmem(T1, R1),
                vmem(2, T2, R2), vmem(T2, R2), vmem(T2, R2), vmem(2, 1, T2, R2), vmem(T2, R2), vmem(T2, R2),
                vmem(T2, R2),
                vmem(T3, R3), vmem(T3, R3), vmem(T3, R3), vmem(T3, R3),
                vmem(2, 2, R0), vmem(2, 1, R1), vmem(2, 2, R2), vmem(2, 2, 1, R2), vmem(2, 2, 2, R1),
                vmem(2, 2, T1, R1),
                pltpu.SemaphoreType.DMA((4, T0 - 1)), pltpu.SemaphoreType.DMA((2, T0 - 1)),
                pltpu.SemaphoreType.DMA((7, 8)), pltpu.SemaphoreType.DMA((7, 8)),
            ],
            compiler_params=pltpu.CompilerParams(
                collective_id=0, has_side_effects=True, vmem_limit_bytes=48 * 1024 * 1024),
        )(guide, screen, valid, tiles)

    spec = P("lat", "lon")
    return jax.shard_map(
        body, mesh=mesh, in_specs=(spec,) * 4, out_specs=(spec,) * 2, check_vma=False)
```

```python
import functools

import jax
import jax.numpy as jnp
from jax import lax
from jax.experimental import pallas as pl
from jax.experimental.pallas import tpu as pltpu
from jax.sharding import PartitionSpec as P

OMEGA = 0.8
MESH = pl.DeviceIdType.MESH
LANES = 128

T0, O0, N0 = 9, 24, 128
T1, O1, N1 = 5, 16, 64
T2, O2, N2 = 3, 32, 32
T3, O3, N3 = 2, 20, 16
R0, R1, R2, R3 = 176, 96, 96, 56
A0, A1, A2, A3 = (8, 168), (8, 88), (8, 88), (8, 48)
H0, H1, H2 = 16, 8, 24
DIRS = ((-1, 0), (1, 0), (0, -1), (0, 1), (-1, -1), (-1, 1), (1, -1), (1, 1))


def lanes_of(x):
    return lax.broadcasted_iota(jnp.int32, x.shape, 1)


def neighbours(src, t, count, lo, hi):
    x = src[t, lo:hi]
    lane = lanes_of(x)
    left = pltpu.roll(jnp.where(lane == LANES - 1, src[(t - 1) % count, lo:hi], x), 1, 1)
    right = pltpu.roll(jnp.where(lane == 0, src[(t + 1) % count, lo:hi], x), LANES - 1, 1)
    return x, ((src[t, lo - 1:hi - 1] + src[t, lo + 1:hi + 1]) + left) + right


def sweep(src, dst, g, b, count, lo, hi):
    for t in range(count):
        x, near = neighbours(src, t, count, lo, hi)
        dst[t, lo:hi] = (1.0 - OMEGA) * x + b[t, lo:hi] * (g[t, lo:hi] + near)


def first_sweep(dst, g, b, count, lo, hi):
    for t in range(count):
        dst[t, lo:hi] = b[t, lo:hi] * g[t, lo:hi]


def residual_of(src, dst, g, e, count, lo, hi, tiles):
    for t in range(tiles):
        x, near = neighbours(src, t, count, lo, hi)
        ee = e[t, lo:hi]
        dst[t, lo:hi] = jnp.where(ee > 0.0, (g[t, lo:hi] + near) - ee * x, 0.0)


def gather(x, index):
    return jnp.take_along_axis(x, index, axis=1, mode="promise_in_bounds")


def coarsen(src, t, tiles, lo, rows, op):
    def pair(tile):
        return op(src[tile, pl.ds(lo, rows, stride=2)], src[tile, pl.ds(lo + 1, rows, stride=2)])

    x = pair(2 * t)
    lane = lanes_of(x)
    x = op(x, pltpu.roll(x, LANES - 1, 1))
    if 2 * t + 1 < tiles:
        y = pair(2 * t + 1)
        x = jnp.where(lane % 2 == 0, x, op(y, pltpu.roll(y, 1, 1)))
        index = jnp.where(lane < LANES // 2, 2 * lane, 2 * lane - (LANES - 1))
    else:
        index = (2 * lane) % LANES
    return gather(x, index)


def correct(coarse, fine, e, count, clo, rows, lo):
    for t in range(count):
        c = coarse[t // 2, clo:clo + rows]
        lane = lanes_of(c)
        half = lane // 2
        if t == count - 1:
            index = jnp.where(lane < LANES // 2, half, LANES // 2 + half)
        else:
            index = half + (LANES // 2) * (t % 2)
        c = gather(c, index)
        for odd in range(2):
            rws = pl.ds(lo + odd, rows, stride=2)
            fine[t, rws] = fine[t, rws] + jnp.where(e[t, rws] > 0.0, c, 0.0)


def kernel(lon_count, lat_count, guide, screen, valid, tiles, out, res,
           gin, win, vin, fin, sb, e0, v0, w0, r0, vg, bb, e1, u1, r1, wa, b2, e2, gg, v2, u2, r2, b3, g3, v3, u3,
           xsb, xbb, xwa, xgg, xvg, rvg, in_sem, out_sem, send_sem, recv_sem):
    lon = lax.axis_index("lon")
    lat = lax.axis_index("lat")
    s0, b0 = sb.at[0], sb.at[1]
    v1, g1, b1 = vg.at[0], vg.at[1], bb.at[0]
    w2, a2 = wa.at[0], wa.at[1]

    loads = []
    for i, (src, dst) in enumerate(((screen, win), (valid, vin), (guide, gin))):
        for t in range(T0 - 1):
            loads.append(pltpu.make_async_copy(src.at[:, pl.ds(t * LANES, LANES)], dst.at[t], in_sem.at[i, t]))
    flag_copy = pltpu.make_async_copy(tiles, fin, in_sem.at[3, 0])

    def peer(d):
        return {"lat": lax.rem(lat + DIRS[d][0] + lat_count, lat_count), "lon": lax.rem(lon + DIRS[d][1] + lon_count, lon_count)}

    def exists(d):
        if DIRS[d][0] < 0:
            return lat > 0
        if DIRS[d][0] > 0:
            return lat < lat_count - 1
        return None

    def guarded(condition, fn):
        if condition is None:
            fn()
        else:
            pl.when(condition)(fn)

    barrier = pltpu.get_barrier_semaphore()
    for d in range(8):
        guarded(exists(d), lambda d=d: pl.semaphore_signal(
            barrier, inc=1, device_id=peer(d), device_id_type=MESH))

    flag_copy.start()
    for copy in loads:
        copy.start()
    for ref, rows, lo, hi in ((v0, R0, *A0), (w0, R0, *A0), (v1, R1, *A1), (u1, R1, *A1), (v2, R2, *A2),
                              (u2, R2, *A2), (v3, R3, *A3), (u3, R3, *A3)):
        zero = jnp.zeros((ref.shape[0], 8, LANES), jnp.float32)
        ref[:, lo - 8:lo] = zero
        ref[:, hi:hi + 8] = zero

    interior = jnp.logical_and(lat > 0, lat < lat_count - 1).astype(jnp.int32)
    pl.semaphore_wait(barrier, 5 + 3 * interior)

    def message(kind, d, src, rows_dst, land, count, first, rows, depth):
        dy, dx = DIRS[d]
        if dy < 0:
            from_rows, to_rows = pl.ds(first, depth), pl.ds(first + rows, depth)
        elif dy > 0:
            from_rows, to_rows = pl.ds(first + rows - depth, depth), pl.ds(first - depth, depth)
        else:
            from_rows = to_rows = pl.ds(first, rows)
        if dx == 0:
            src = src.at[:, pl.ds(0, count - 1), from_rows]
            dst = rows_dst.at[:, pl.ds(0, count - 1), to_rows]
        else:
            src = src.at[:, 0 if dx < 0 else count - 2, from_rows]
            dst = land.at[1 if dx < 0 else 0, :, to_rows]
        return pltpu.make_async_remote_copy(
            src_ref=src, dst_ref=dst, send_sem=send_sem.at[kind, d], recv_sem=recv_sem.at[kind, d],
            device_id=peer(d), device_id_type=MESH)

    def send(kind, *where):
        for d in range(8):
            guarded(exists(d), lambda d=d: message(kind, d, *where).start())

    def sent(kind, *where):
        for d in range(8):
            guarded(exists(d), lambda d=d: message(kind, d, *where).wait_send())

    def received(kind, *where):
        src, rows_dst, land, count, first, rows, depth = where
        for d in range(8):
            back = DIRS.index((-DIRS[d][0], -DIRS[d][1]))
            guarded(exists(back), lambda d=d: message(kind, d, *where).wait_recv())
        for outside, lo in ((lat == 0, first - depth), (lat == lat_count - 1, first + rows)):
            @pl.when(outside)
            def _():
                for k in range(rows_dst.shape[0]):
                    rows_dst[k, :, lo:lo + depth] = jnp.zeros((rows_dst.shape[1], depth, LANES), jnp.float32)
                    for side in range(2):
                        land[side, k, lo:lo + depth] = jnp.zeros((depth, LANES), jnp.float32)

    def merge(land, k, ref, count, lo, hi):
        left = land[0, k, lo:hi]
        ref[count - 1, lo:hi] = jnp.where(lanes_of(left) < LANES // 2, land[1, k, lo:hi], left)

    flag_copy.wait()
    for copy in loads:
        copy.wait()
    own = slice(O0, O0 + N0)
    for t in range(T0 - 1):
        active = vin[t].astype(jnp.float32) * fin[0, t].astype(jnp.float32)
        diag = 4.0 + win[t]
        s0[t, own] = active * gin[t]
        b0[t, own] = active * OMEGA / diag
        e0[t, own] = active * diag
        r0[t, own] = active
    msg0 = (0, sb, sb, xsb, T0, O0, N0, H0)
    send(*msg0)

    own1 = slice(O1, O1 + N1)
    for t in range(T1 - 1):
        active = coarsen(r0, t, T0 - 1, O0, N1, jnp.maximum)
        weight = coarsen(win, t, T0 - 1, 0, N1, jnp.add)
        diag = 4.0 + weight
        b1[t, own1] = active * OMEGA / diag
        e1[t, own1] = active * diag
        r1[t, own1] = active
        u1[t, own1] = weight
    msg1 = (1, bb, bb, xbb, T1, O1, N1, H1)
    send(*msg1)

    for t in range(T2 - 1):
        a2[t, O2:O2 + N2] = coarsen(r1, t, T1 - 1, O1, N2, jnp.maximum)
        w2[t, O2:O2 + N2] = coarsen(u1, t, T1 - 1, O1, N2, jnp.add)
    msg2 = (2, wa, wa, xwa, T2, O2, N2, H2)
    send(*msg2)

    def masked_inverse(x):
        return jnp.where(x > 0.0, OMEGA / jnp.where(x > 0.0, x, 1.0), 0.0)

    received(*msg0)
    for k in range(2):
        merge(xsb, k, sb.at[k], T0, *A0)
    for t in range(T0):
        for lo, hi in (A0,) if t == T0 - 1 else ((A0[0], O0), (O0 + N0, A0[1])):
            e0[t, lo:hi] = masked_inverse(b0[t, lo:hi])

    for cycle in range(2):
        g2 = gg.at[cycle, 0]
        if cycle == 0:
            first_sweep(w0, s0, b0, T0, *A0)
        else:
            sweep(v0, w0, s0, b0, T0, *A0)
        sweep(w0, v0, s0, b0, T0, *A0)
        residual_of(v0, r0, s0, e0, T0, *A0, T0)

        if cycle == 0:
            received(*msg1)
            merge(xbb, 0, b1, T1, *A1)
        for t in range(T1):
            g1[t, A1[0]:A1[1]] = jnp.where(
                b1[t, A1[0]:A1[1]] > 0.0, coarsen(r0, t, T0, A0[0], A1[1] - A1[0], jnp.add), 0.0)
        first_sweep(u1, g1, b1, T1, *A1)
        sweep(u1, v1, g1, b1, T1, *A1)
        residual_of(v1, r1, g1, e1, T1, O1, O1 + N1, T1 - 1)
        for t in range(T2 - 1):
            g2[t, O2:O2 + N2] = jnp.where(
                a2[t, O2:O2 + N2] > 0.0, coarsen(r1, t, T1 - 1, O1, N2, jnp.add), 0.0)
        msg_g = (3 + 2 * cycle, gg.at[cycle], gg.at[cycle], xgg.at[cycle], T2, O2, N2, H2)
        msg_v = (4 + 2 * cycle, vg, rvg.at[cycle], xvg.at[cycle], T1, O1, N1, H1)
        send(*msg_g)
        send(*msg_v)

        if cycle == 0:
            received(*msg2)
            for k in range(2):
                merge(xwa, k, wa.at[k], T2, *A2)
            for t in range(T2):
                lo, hi = A2
                diag = 4.0 + w2[t, lo:hi]
                b2[t, lo:hi] = a2[t, lo:hi] * OMEGA / diag
                e2[t, lo:hi] = a2[t, lo:hi] * diag
            for t in range(T3):
                lo, hi = A3
                b3[t, lo:hi] = coarsen(a2, t, T2, A2[0], hi - lo, jnp.maximum) * OMEGA / (
                    4.0 + coarsen(w2, t, T2, A2[0], hi - lo, jnp.add))
        received(*msg_g)
        merge(xgg.at[cycle], 0, g2, T2, *A2)
        first_sweep(u2, g2, b2, T2, *A2)
        sweep(u2, v2, g2, b2, T2, *A2)
        residual_of(v2, r2, g2, e2, T2, *A2, T2)
        for t in range(T3):
            lo, hi = A3
            g3[t, lo:hi] = jnp.where(b3[t, lo:hi] > 0.0, coarsen(r2, t, T2, A2[0], hi - lo, jnp.add), 0.0)
        first_sweep(v3, g3, b3, T3, *A3)
        for i in range(7):
            src, dst = (v3, u3) if i % 2 == 0 else (u3, v3)
            sweep(src, dst, g3, b3, T3, *A3)
        correct(u3, v2, e2, T2, A3[0], A3[1] - A3[0], A2[0])
        sweep(v2, u2, g2, b2, T2, *A2)
        sweep(u2, v2, g2, b2, T2, *A2)
        sent(*msg_g)

        sent(*msg_v)
        received(*msg_v)
        for k in range(2):
            for t in range(T1 - 1):
                for lo, hi in ((A1[0], O1), (O1 + N1, A1[1])):
                    vg[k, t, lo:hi] = rvg[cycle, k, t, lo:hi]
            merge(xvg.at[cycle], k, vg.at[k], T1, *A1)
        correct(v2, v1, b1, T1, O2 - 4, 40, A1[0])
        sweep(v1, u1, g1, b1, T1, *A1)
        sweep(u1, v1, g1, b1, T1, *A1)
        correct(v1, v0, e0, T0, A1[0], A1[1] - A1[0], A0[0])
        sweep(v0, w0, s0, b0, T0, *A0)
        sweep(w0, v0, s0, b0, T0, *A0)

    stores = []
    for i, (src, dst) in enumerate(((v0, out), (r0, res))):
        if i == 1:
            residual_of(v0, r0, s0, e0, T0, O0, O0 + N0, T0 - 1)
        for t in range(T0 - 1):
            stores.append(pltpu.make_async_copy(
                src.at[t, pl.ds(O0, N0)], dst.at[:, pl.ds(t * LANES, LANES)], out_sem.at[i, t]))
            stores[-1].start()
    sent(*msg0)
    sent(*msg1)
    sent(*msg2)
    for copy in stores:
        copy.wait()


def store(a, b, out, res, sem):
    copies = [pltpu.make_async_copy(x, y, sem.at[i]) for i, (x, y) in enumerate(((a, out), (b, res)))]
    for copy in copies:
        copy.start()
    for copy in copies:
        copy.wait()


def solution(mesh):
    def body(guide, screen, valid, tiles):
        def vmem(*shape):
            return pltpu.VMEM(shape + (LANES,), jnp.float32)

        guide, screen, valid, tiles = [
            pltpu.with_memory_space_constraint(x, pltpu.HBM) for x in (guide, screen, valid, tiles)]
        pair = pl.pallas_call(
            functools.partial(kernel, mesh.shape["lon"], mesh.shape["lat"]),
            out_shape=(pltpu.VMEM(guide.shape, jnp.float32),) * 2,
            in_specs=[pl.BlockSpec(memory_space=pl.ANY)] * 4,
            out_specs=(pl.BlockSpec(memory_space=pl.ANY),) * 2,
            scratch_shapes=[
                vmem(T0 - 1, N0), vmem(T0 - 1, N0), pltpu.VMEM((T0 - 1, N0, LANES), jnp.int32),
                pltpu.SMEM((1, T0 - 1), jnp.int32),
                vmem(2, T0, R0), vmem(T0, R0), vmem(T0, R0), vmem(T0, R0), vmem(T0, R0),
                vmem(2, T1, R1), vmem(1, T1, R1), vmem(T1, R1), vmem(T1, R1), vmem(T1, R1),
                vmem(2, T2, R2), vmem(T2, R2), vmem(T2, R2), vmem(2, 1, T2, R2), vmem(T2, R2), vmem(T2, R2),
                vmem(T2, R2),
                vmem(T3, R3), vmem(T3, R3), vmem(T3, R3), vmem(T3, R3),
                vmem(2, 2, R0), vmem(2, 1, R1), vmem(2, 2, R2), vmem(2, 2, 1, R2), vmem(2, 2, 2, R1),
                vmem(2, 2, T1, R1),
                pltpu.SemaphoreType.DMA((4, T0 - 1)), pltpu.SemaphoreType.DMA((2, T0 - 1)),
                pltpu.SemaphoreType.DMA((7, 8)), pltpu.SemaphoreType.DMA((7, 8)),
            ],
            compiler_params=pltpu.CompilerParams(
                collective_id=0, has_side_effects=True, vmem_limit_bytes=48 * 1024 * 1024),
        )(guide, screen, valid, tiles)
        pair = [pltpu.with_memory_space_constraint(x, pltpu.VMEM) for x in pair]
        return pl.pallas_call(
            store,
            out_shape=(pltpu.HBM(guide.shape, jnp.float32),) * 2,
            in_specs=[pl.BlockSpec(memory_space=pl.ANY)] * 2,
            out_specs=(pl.BlockSpec(memory_space=pltpu.HBM),) * 2,
            scratch_shapes=[pltpu.SemaphoreType.DMA((2,))],
        )(*pair)

    spec = P("lat", "lon")
    return jax.shard_map(
        body, mesh=mesh, in_specs=(spec,) * 4, out_specs=(spec,) * 2, check_vma=False)
```

```python
import functools

import jax
import jax.numpy as jnp
from jax import lax
from jax.experimental import pallas as pl
from jax.experimental.pallas import tpu as pltpu
from jax.sharding import PartitionSpec as P

OMEGA = 0.8
MESH = pl.DeviceIdType.MESH
LANES = 128
HALF = LANES // 2

P0, P1, P2, P3 = 4, 2, 1, 1
T0, T1, T2, T3 = 3, 3, 3, 2
O0, O1, O2, O3 = 24, 16, 32, 20
N0, N1, N2, N3 = 128, 64, 32, 16
R0, R1, R2, R3 = 176, 96, 96, 56
A0, B0, A1, A2, A3 = (8, 168), (16, 160), (8, 88), (8, 88), (8, 48)
H0, H1, H2 = 16, 8, 24
OWN = 8
DIRS = ((-1, 0), (1, 0), (0, -1), (0, 1), (-1, -1), (-1, 1), (1, -1), (1, 1))


def lanes_of(x):
    return lax.broadcasted_iota(jnp.int32, x.shape, 1)


def gather(x, index):
    return jnp.take_along_axis(x, index, axis=1, mode="promise_in_bounds")


def barrel(tiles, lane):
    odd, high = (lane & 32) != 0, lane >= HALF
    half = [jnp.where(odd, tiles[(i + 1) % 4], tiles[i]) for i in range(4)]
    return [jnp.where(high, half[(i + 2) % 4], half[i]) for i in range(4)]


def split_phases(sources, mid, rows, store):
    for t, src in enumerate(sources):
        x = src(slice(0, rows))
        lane = lanes_of(x)
        mid[t, 0:rows] = gather(x, ((lane & 31) << 2) + (((lane >> 5) + (4 - t)) & 3))
    for row in range(0, rows, 16):
        part = slice(row, row + 16)
        tiles = [mid[t, part] for t in range(4)]
        mixed = barrel(tiles, lanes_of(tiles[0]))
        store(0, part, mixed[0])
        for p in range(1, 4):
            store(p, part, pltpu.roll(mixed[4 - p], LANES - 32 * p, 1))


def join_phases(sources, mid, rows, stores):
    for row in range(0, rows, 16):
        part = slice(row, row + 16)
        phases = [src(part) for src in sources]
        placed = [phases[0]] + [pltpu.roll(phases[p], 32 * p, 1) for p in range(1, 4)]
        mixed = barrel(placed, lanes_of(placed[0]))
        for t in range(4):
            mid[t, part] = mixed[(4 - t) % 4]
    for t, store in enumerate(stores):
        x = mid[t, 0:rows]
        lane = lanes_of(x)
        store(gather(x, (((lane + t) & 3) << 5) + (lane >> 2)))


def neighbours(src, i, phases, count, lo, hi):
    t, p = i // phases, i % phases
    x = src[i, lo:hi]
    lane = lanes_of(x)
    if p > 0:
        left = src[i - 1, lo:hi]
    else:
        last = phases - 1
        left = pltpu.roll(jnp.where(
            lane == LANES - 1, src[((t - 1) % count) * phases + last, lo:hi], src[t * phases + last, lo:hi]), 1, 1)
    if p < phases - 1:
        right = src[i + 1, lo:hi]
    else:
        right = pltpu.roll(jnp.where(
            lane == 0, src[((t + 1) % count) * phases, lo:hi], src[t * phases, lo:hi]), LANES - 1, 1)
    return x, ((src[i, lo - 1:hi - 1] + src[i, lo + 1:hi + 1]) + left) + right


def sweep(src, dst, g, b, phases, count, lo, hi):
    for i in range(phases * count):
        x, near = neighbours(src, i, phases, count, lo, hi)
        dst[i, lo:hi] = (1.0 - OMEGA) * x + b[i, lo:hi] * (g[i, lo:hi] + near)


def first_sweep(dst, g, b, planes, lo, hi):
    for i in range(planes):
        dst[i, lo:hi] = b[i, lo:hi] * g[i, lo:hi]


def residual_of(src, g, e, i, phases, count, lo, hi):
    x, near = neighbours(src, i, phases, count, lo, hi)
    ee = e[i, lo:hi]
    return jnp.where(ee > 0.0, (g[i, lo:hi] + near) - ee * x, 0.0)


def rows_op(src, i, lo, rows, op):
    return op(src[i, pl.ds(lo, rows, stride=2)], src[i, pl.ds(lo + 1, rows, stride=2)])


def restrict(src, g, e, phases, count, planes, lo, hi, tmp, out, active, tlo, olo, rows):
    for i in range(planes):
        tmp[i, lo:hi] = residual_of(src, g, e, 2 * i, phases, count, lo, hi) + residual_of(
            src, g, e, 2 * i + 1, phases, count, lo, hi)
    for i in range(planes):
        out[i, olo:olo + rows] = jnp.where(
            active[i, olo:olo + rows] > 0.0, rows_op(tmp, i, tlo, rows, jnp.add), 0.0)


def coarsen(src, i, lo, rows, op):
    return op(rows_op(src, 2 * i, lo, rows, op), rows_op(src, 2 * i + 1, lo, rows, op))


def correct(coarse, fine, b, planes, clo, rows, lo, tmp):
    hi = lo + 2 * rows
    for i in range(planes):
        c = coarse[i, clo:clo + rows]
        tmp[i, pl.ds(lo, rows, stride=2)] = c
        tmp[i, pl.ds(lo + 1, rows, stride=2)] = c
    for i in range(2 * planes):
        fine[i, lo:hi] = fine[i, lo:hi] + jnp.where(b[i, lo:hi] > 0.0, tmp[i // 2, lo:hi], 0.0)


def pack(src, t, lo, rows, op):
    x = rows_op(src, 2 * t, lo, rows, op)
    lane = lanes_of(x)
    x = op(x, pltpu.roll(x, LANES - 1, 1))
    if 2 * t + 1 < T2:
        y = rows_op(src, 2 * t + 1, lo, rows, op)
        x = jnp.where((lane & 1) == 0, x, op(y, pltpu.roll(y, 1, 1)))
        index = jnp.where(lane < HALF, 2 * lane, 2 * lane - (LANES - 1))
    else:
        index = (2 * lane) & (LANES - 1)
    return gather(x, index)


def unpack(coarse, fine, b, clo, rows, lo, tmp):
    hi = lo + 2 * rows
    for t in range(T2):
        c = coarse[t // 2, clo:clo + rows]
        lane = lanes_of(c)
        if t == T2 - 1:
            index = (lane >> 1) + jnp.where(lane < HALF, 0, HALF)
        else:
            index = (lane >> 1) + HALF * (t % 2)
        c = gather(c, index)
        tmp[t, pl.ds(lo, rows, stride=2)] = c
        tmp[t, pl.ds(lo + 1, rows, stride=2)] = c
    for t in range(T2):
        fine[t, lo:hi] = fine[t, lo:hi] + jnp.where(b[t, lo:hi] > 0.0, tmp[t, lo:hi], 0.0)


def masked_inverse(x):
    return jnp.where(x > 0.0, OMEGA / jnp.where(x > 0.0, x, 1.0), 0.0)


def kernel(lon_count, lat_count, guide, screen, valid, tiles, out, res,
           gin, win, vin, fin, nat, mid, s0, b0, e0, v0, w0, tmp, vg, bb, e1, u1, wa, b2, e2, gg, v2, u2, r2, b3, g3, v3, u3,
           xbb, xwa, rvg, in_sem, out_sem, send_sem, recv_sem):
    lon = lax.axis_index("lon")
    lat = lax.axis_index("lat")
    v1, g1, b1 = vg.at[0], vg.at[1], bb.at[0]
    w2, a2 = wa.at[0], wa.at[1]
    n0, n1, n2, n3 = P0 * T0, P1 * T1, P2 * T2, P3 * T3

    def peer(d):
        return {"lat": lax.rem(lat + DIRS[d][0] + lat_count, lat_count),
                "lon": lax.rem(lon + DIRS[d][1] + lon_count, lon_count)}

    def exists(dy):
        return lat > 0 if dy < 0 else lat < lat_count - 1 if dy > 0 else None

    def guarded(condition, fn):
        if condition is None:
            fn()
        else:
            pl.when(condition)(fn)

    barrier = pltpu.get_barrier_semaphore()
    for d in range(8):
        guarded(exists(DIRS[d][0]), lambda d=d: pl.semaphore_signal(
            barrier, inc=1, device_id=peer(d), device_id_type=MESH))

    loads = [pltpu.make_async_copy(src, dst, in_sem.at[i]) for i, (src, dst) in enumerate((
        (valid, vin), (screen, win), (guide, gin), (tiles, fin)))]
    for copy in loads:
        copy.start()

    for ref, lo, hi in ((v0, *A0), (w0, *A0), (v1, *A1), (u1, *A1), (v2, *A2), (u2, *A2), (v3, *A3), (u3, *A3)):
        zero = jnp.zeros((ref.shape[0], 8, LANES), jnp.float32)
        ref[:, lo - 8:lo] = zero
        ref[:, hi:hi + 8] = zero

    def copy_of(message, d):
        kind, parts = message
        src, dst = parts[d]
        return pltpu.make_async_remote_copy(
            src_ref=src, dst_ref=dst, send_sem=send_sem.at[kind, d], recv_sem=recv_sem.at[kind, d],
            device_id=peer(d), device_id_type=MESH)

    def send(message):
        for d in message[1]:
            guarded(exists(DIRS[d][0]), lambda d=d: copy_of(message, d).start())

    def sent(message):
        for d in message[1]:
            guarded(exists(DIRS[d][0]), lambda d=d: copy_of(message, d).wait_send())

    def received(message):
        for d in message[1]:
            guarded(exists(-DIRS[d][0]), lambda d=d: copy_of(message, d).wait_recv())

    def clear(refs, above, below):
        for edge, rows in ((lat == 0, above), (lat == lat_count - 1, below)):
            @pl.when(edge)
            def _():
                for ref in refs:
                    zero = jnp.zeros((rows[1] - rows[0], LANES), jnp.float32)
                    for i in range(ref.shape[0]):
                        ref[i, rows[0]:rows[1]] = zero

    def row_spans(dy, first, rows, depth, skip=0):
        if dy < 0:
            return pl.ds(first + skip, depth), pl.ds(first + rows + skip, depth)
        if dy > 0:
            return pl.ds(first + rows - depth - skip, depth), pl.ds(first - depth - skip, depth)
        return (pl.ds(first, rows),) * 2

    first_parts, far_parts = {}, {}
    for d, (dy, dx) in enumerate(DIRS):
        if dx == 0:
            own = pl.ds(0, OWN)
            for parts, skip in ((first_parts, 0), (far_parts, 8)):
                a, b = row_spans(dy, H0, N0, 8, skip)
                parts[d] = nat.at[:, own, a], nat.at[:, own, b]
        else:
            a, b = row_spans(dy, H0, N0, H0)
            mine, theirs = (0, OWN) if dx < 0 else (OWN - 2, OWN + 2)
            first_parts[d] = nat.at[:, pl.ds(mine, 2), a], nat.at[:, pl.ds(theirs, 2), b]
    first_message, far_message = (0, first_parts), (1, far_parts)

    def coarse_parts(ref, land, phases, first, rows, depth):
        parts = {}
        for d, (dy, dx) in enumerate(DIRS):
            a, b = row_spans(dy, first, rows, depth)
            if dx == 0:
                own = pl.ds(0, 2 * phases)
                parts[d] = ref.at[:, own, a], ref.at[:, own, b]
            else:
                mine, side = (0, 1) if dx < 0 else (phases, 0)
                parts[d] = ref.at[:, pl.ds(mine, phases), a], land.at[side, :, :, b]
        return parts

    def row_parts(src, dst, first, rows, depth):
        parts = {}
        for d in range(2):
            a, b = row_spans(DIRS[d][0], first, rows, depth)
            parts[d] = src.at[..., a, :], dst.at[..., b, :]
        return parts

    def merge(land, k, ref, phases, lo, hi):
        for p in range(phases):
            left = land[0, k, p, lo:hi]
            ref[2 * phases + p, lo:hi] = jnp.where(lanes_of(left) < HALF, land[1, k, p, lo:hi], left)

    for copy in loads:
        copy.wait()
    for t in range(OWN):
        cols = slice(t * LANES, (t + 1) * LANES)
        active = vin[:, cols].astype(jnp.float32) * fin[0, t].astype(jnp.float32)
        nat[0, t, H0:H0 + N0] = active * gin[:, cols]
        nat[1, t, H0:H0 + N0] = active * OMEGA / (4.0 + win[:, cols])
    interior = jnp.logical_and(lat > 0, lat < lat_count - 1).astype(jnp.int32)
    pl.semaphore_wait(barrier, 5 + 3 * interior)
    send(first_message)
    send(far_message)

    def arrange(t, lo, hi):
        for k, ref in enumerate((s0, b0)):
            def store(p, part, x, ref=ref):
                ref[P0 * t + p, lo + O0 - H0 + part.start:lo + O0 - H0 + part.stop] = x

            split_phases([lambda part, j=j: nat[k, 4 * t + j, lo + part.start:lo + part.stop] for j in range(4)],
                         mid.at[k], hi - lo, store)

    def columns(t):
        return slice(t * LANES, (t + 1) * LANES)

    for t in range(2):
        arrange(t, H0, H0 + N0)

        def store_weight(p, part, x):
            w0[P0 * t + p, part.start + O0:part.stop + O0] = x

        split_phases([lambda part, j=j: win[part, columns(4 * t + j)] for j in range(4)], mid.at[0], N0, store_weight)
    own = slice(O0, O0 + N0)
    for i in range(2 * P0):
        on = b0[i, own] > 0.0
        e0[i, own] = jnp.where(on, 4.0 + w0[i, own], 0.0)
        v0[i, own] = jnp.where(on, 1.0, 0.0)

    own = slice(O1, O1 + N1)
    for i in range(2 * P1):
        active = coarsen(v0, i, O0, N1, jnp.maximum)
        weight = coarsen(w0, i, O0, N1, jnp.add)
        diag = 4.0 + weight
        b1[i, own] = active * OMEGA / diag
        v1[i, own] = active
        u1[i, own] = weight
    message1 = (2, coarse_parts(bb, xbb, P1, O1, N1, H1))
    send(message1)

    for i in range(2 * P2):
        w2[i, O2:O2 + N2] = coarsen(u1, i, O1, N2, jnp.add)
        a2[i, O2:O2 + N2] = coarsen(v1, i, O1, N2, jnp.maximum)
    message2 = (3, coarse_parts(wa, xwa, P2, O2, N2, H2))
    send(message2)

    received(first_message)
    received(far_message)
    clear((nat.at[0], nat.at[1]), (0, H0), (H0 + N0, 2 * H0 + N0))
    for t in range(T0):
        for lo, hi in ((0, 2 * H0 + N0),) if t == T0 - 1 else ((0, H0), (H0 + N0, 2 * H0 + N0)):
            arrange(t, lo, hi)
            for i in range(P0 * t, P0 * t + P0):
                e0[i, lo + 8:hi + 8] = masked_inverse(b0[i, lo + 8:hi + 8])

    for cycle in range(2):
        rows0 = A0 if cycle == 0 else B0
        g2 = gg.at[cycle]
        if cycle == 0:
            first_sweep(w0, s0, b0, n0, *rows0)
        else:
            sweep(v0, w0, s0, b0, P0, T0, *rows0)
        sweep(w0, v0, s0, b0, P0, T0, *rows0)

        if cycle == 0:
            received(message1)
            clear((bb.at[0], xbb.at[0, 0], xbb.at[1, 0]), (O1 - H1, O1), (O1 + N1, O1 + N1 + H1))
            merge(xbb, 0, b1, P1, *A1)
            for i in range(n1):
                e1[i, A1[0]:A1[1]] = masked_inverse(b1[i, A1[0]:A1[1]])
        restrict(v0, s0, e0, P0, T0, n1, *B0, tmp, g1, b1, A0[0], A1[0], A1[1] - A1[0])
        first_sweep(u1, g1, b1, n1, *A1)
        sweep(u1, v1, g1, b1, P1, T1, *A1)
        if cycle == 0:
            received(message2)
            clear((w2, a2, xwa.at[0, 0], xwa.at[0, 1], xwa.at[1, 0], xwa.at[1, 1]),
                  (O2 - H2, O2), (O2 + N2, O2 + N2 + H2))
            for k in range(2):
                merge(xwa, k, wa.at[k], P2, *A2)
        restrict(v1, g1, e1, P1, T1, n2, O1, O1 + N1, tmp, g2, a2, O1, O2, N2)
        message_g = (4 + cycle, row_parts(g2, g2, O2, N2, H2))
        message_v = (6 + cycle, row_parts(vg, rvg.at[cycle], O1, N1, H1))
        send(message_g)
        send(message_v)

        if cycle == 0:
            lo, hi = A2
            for t in range(n2):
                diag = 4.0 + w2[t, lo:hi]
                b2[t, lo:hi] = a2[t, lo:hi] * OMEGA / diag
                e2[t, lo:hi] = a2[t, lo:hi] * diag
            lo, hi = A3
            for t in range(n3):
                b3[t, lo:hi] = pack(a2, t, A2[0], hi - lo, jnp.maximum) * OMEGA / (
                    4.0 + pack(w2, t, A2[0], hi - lo, jnp.add))
        received(message_g)
        clear((g2,), (O2 - H2, O2), (O2 + N2, O2 + N2 + H2))
        first_sweep(u2, g2, b2, n2, *A2)
        sweep(u2, v2, g2, b2, P2, T2, *A2)
        for t in range(n2):
            r2[t, A2[0]:A2[1]] = residual_of(v2, g2, e2, t, P2, T2, *A2)
        lo, hi = A3
        for t in range(n3):
            g3[t, lo:hi] = jnp.where(b3[t, lo:hi] > 0.0, pack(r2, t, A2[0], hi - lo, jnp.add), 0.0)
        first_sweep(v3, g3, b3, n3, *A3)
        for i in range(7):
            src, dst = (v3, u3) if i % 2 == 0 else (u3, v3)
            sweep(src, dst, g3, b3, P3, T3, *A3)
        unpack(u3, v2, b2, A3[0], hi - lo, A2[0], tmp)
        sweep(v2, u2, g2, b2, P2, T2, *A2)
        sweep(u2, v2, g2, b2, P2, T2, *A2)

        sent(message_g)
        sent(message_v)
        received(message_v)
        clear((rvg.at[cycle, 0], rvg.at[cycle, 1]), (O1 - H1, O1), (O1 + N1, O1 + N1 + H1))
        for k in range(2):
            for i in range(n1):
                for lo, hi in ((A1[0], O1), (O1 + N1, A1[1])):
                    vg[k, i, lo:hi] = rvg[cycle, k, i, lo:hi]
        correct(v2, v1, b1, n2, O2 - 4, (A1[1] - A1[0]) // 2, A1[0], tmp)
        sweep(v1, u1, g1, b1, P1, T1, *A1)
        sweep(u1, v1, g1, b1, P1, T1, *A1)
        correct(v1, v0, b0, n1, A1[0], A1[1] - A1[0], A0[0], tmp)
        sweep(v0, w0, s0, b0, P0, T0, *rows0)
        sweep(w0, v0, s0, b0, P0, T0, *rows0)

    stores = []
    for k, (stage, dst) in enumerate(((gin, out), (win, res))):
        if k == 1:
            for i in range(2 * P0):
                w0[i, O0:O0 + N0] = residual_of(v0, s0, e0, i, P0, T0, O0, O0 + N0)
        src = w0 if k == 1 else v0
        for t in range(2):
            def store_tile(j, x):
                stage[:, columns(4 * t + j)] = x

            join_phases([lambda part, p=p: src[P0 * t + p, part.start + O0:part.stop + O0] for p in range(P0)],
                        mid.at[t], N0, [functools.partial(store_tile, j) for j in range(4)])
        stores.append(pltpu.make_async_copy(stage, dst, out_sem.at[k]))
        stores[-1].start()
    for message in (first_message, far_message, message1, message2):
        sent(message)
    for copy in stores:
        copy.wait()


def store(a, b, out, res, sem):
    copies = [pltpu.make_async_copy(x, y, sem.at[i]) for i, (x, y) in enumerate(((a, out), (b, res)))]
    for copy in copies:
        copy.start()
    for copy in copies:
        copy.wait()


def solution(mesh):
    def body(guide, screen, valid, tiles):
        def vmem(*shape):
            return pltpu.VMEM(shape + (LANES,), jnp.float32)

        n0, n1, n2, n3 = P0 * T0, P1 * T1, P2 * T2, P3 * T3
        block = guide.shape
        guide, screen, valid, tiles = [
            pltpu.with_memory_space_constraint(x, pltpu.HBM) for x in (guide, screen, valid, tiles)]
        pair = pl.pallas_call(
            functools.partial(kernel, mesh.shape["lon"], mesh.shape["lat"]),
            out_shape=(pltpu.VMEM(block, jnp.float32),) * 2,
            in_specs=[pl.BlockSpec(memory_space=pl.ANY)] * 4,
            out_specs=(pl.BlockSpec(memory_space=pl.ANY),) * 2,
            scratch_shapes=[
                pltpu.VMEM(block, jnp.float32), pltpu.VMEM(block, jnp.float32), pltpu.VMEM(block, jnp.int32),
                pltpu.SMEM((1, OWN), jnp.int32),
                vmem(2, OWN + 4, N0 + 2 * H0), vmem(2, 4, N0 + 2 * H0), vmem(n0, R0), vmem(n0, R0), vmem(n0, R0), vmem(n0, R0), vmem(n0, R0),
                vmem(n1, R0),
                vmem(2, n1, R1), vmem(1, n1, R1), vmem(n1, R1), vmem(n1, R1),
                vmem(2, n2, R2), vmem(n2, R2), vmem(n2, R2), vmem(2, n2, R2), vmem(n2, R2), vmem(n2, R2), vmem(n2, R2),
                vmem(n3, R3), vmem(n3, R3), vmem(n3, R3), vmem(n3, R3),
                vmem(2, 1, P1, R1), vmem(2, 2, P2, R2), vmem(2, 2, n1, R1),
                pltpu.SemaphoreType.DMA((4,)), pltpu.SemaphoreType.DMA((2,)),
                pltpu.SemaphoreType.DMA((8, 8)), pltpu.SemaphoreType.DMA((8, 8)),
            ],
            compiler_params=pltpu.CompilerParams(
                collective_id=0, has_side_effects=True, vmem_limit_bytes=48 * 1024 * 1024),
        )(guide, screen, valid, tiles)
        pair = [pltpu.with_memory_space_constraint(x, pltpu.VMEM) for x in pair]
        return pl.pallas_call(
            store,
            out_shape=(pltpu.HBM(block, jnp.float32),) * 2,
            in_specs=[pl.BlockSpec(memory_space=pl.ANY)] * 2,
            out_specs=(pl.BlockSpec(memory_space=pltpu.HBM),) * 2,
            scratch_shapes=[pltpu.SemaphoreType.DMA((2,))],
        )(*pair)

    spec = P("lat", "lon")
    return jax.shard_map(
        body, mesh=mesh, in_specs=(spec,) * 4, out_specs=(spec,) * 2, check_vma=False)
```

```python
import functools

import jax
import jax.numpy as jnp
from jax import lax
from jax.experimental import pallas as pl
from jax.experimental.pallas import tpu as pltpu
from jax.sharding import PartitionSpec as P

OMEGA = 0.8
MESH = pl.DeviceIdType.MESH
LANES = 128
CHUNK = 48
HALF = LANES // 2

P0, P1, P2, P3 = 4, 2, 1, 1
T0, T1, T2, T3 = 3, 3, 3, 2
O0, O1, O2, O3 = 24, 16, 32, 20
N0, N1, N2, N3 = 128, 64, 32, 16
R0, R1, R2, R3 = 176, 96, 96, 56
A0, B0, A1, A2, A3 = (8, 168), (16, 160), (8, 88), (8, 88), (8, 48)
H0, H1, H2 = 16, 8, 24
OWN = 8
DIRS = ((-1, 0), (1, 0), (0, -1), (0, 1), (-1, -1), (-1, 1), (1, -1), (1, 1))


def lanes_of(x):
    return lax.broadcasted_iota(jnp.int32, x.shape, 1)


def gather(x, index):
    return jnp.take_along_axis(x, index, axis=1, mode="promise_in_bounds")


def barrel(tiles, lane):
    odd, high = (lane & 32) != 0, lane >= HALF
    half = [jnp.where(odd, tiles[(i + 1) % 4], tiles[i]) for i in range(4)]
    return [jnp.where(high, half[(i + 2) % 4], half[i]) for i in range(4)]


def split_phases(sources, mid, rows, store):
    for t, src in enumerate(sources):
        x = src(slice(0, rows))
        lane = lanes_of(x)
        mid[t, 0:rows] = gather(x, ((lane & 31) << 2) + (((lane >> 5) + (4 - t)) & 3))
    step = min(rows, 16)
    for row in range(0, rows, step):
        part = slice(row, row + step)
        tiles = [mid[t, part] for t in range(4)]
        mixed = barrel(tiles, lanes_of(tiles[0]))
        store(0, part, mixed[0])
        for p in range(1, 4):
            store(p, part, pltpu.roll(mixed[4 - p], LANES - 32 * p, 1))


def join_phases(sources, mid, rows, stores):
    for row in range(0, rows, 16):
        part = slice(row, row + 16)
        phases = [src(part) for src in sources]
        placed = [phases[0]] + [pltpu.roll(phases[p], 32 * p, 1) for p in range(1, 4)]
        mixed = barrel(placed, lanes_of(placed[0]))
        for t in range(4):
            mid[t, part] = mixed[(4 - t) % 4]
    for t, store in enumerate(stores):
        x = mid[t, 0:rows]
        lane = lanes_of(x)
        store(gather(x, (((lane + t) & 3) << 5) + (lane >> 2)))


def neighbours(src, t, phases, count, lo, hi, wanted):
    base, last = t * phases, phases - 1
    row = [src[base + p, lo:hi] for p in range(phases)]
    lane = lanes_of(row[0])
    left = right = None
    if 0 in wanted:
        left = pltpu.roll(jnp.where(lane == LANES - 1, src[((t - 1) % count) * phases + last, lo:hi], row[last]), 1, 1)
    if last in wanted:
        right = pltpu.roll(jnp.where(lane == 0, src[((t + 1) % count) * phases, lo:hi], row[0]), LANES - 1, 1)
    row = [left] + row + [right]
    return [(p, row[p + 1], ((src[base + p, lo - 1:hi - 1] + src[base + p, lo + 1:hi + 1]) + row[p]) + row[p + 2])
            for p in wanted]


def everything(phases, count):
    return {t: tuple(range(phases)) for t in range(count)}


def sweep(src, dst, g, b, phases, count, lo, hi, wanted=None):
    wanted = wanted or everything(phases, count)
    for start in range(lo, hi, CHUNK):
        part = slice(start, min(start + CHUNK, hi))
        for t in wanted:
            for p, x, near in neighbours(src, t, phases, count, part.start, part.stop, wanted[t]):
                i = t * phases + p
                dst[i, part] = (1.0 - OMEGA) * x + b[i, part] * (g[i, part] + near)


def first_sweep(dst, g, b, planes, lo, hi):
    for i in planes:
        dst[i, lo:hi] = b[i, lo:hi] * g[i, lo:hi]


def residual_of(src, g, e, t, phases, count, lo, hi, wanted):
    found = []
    for p, x, near in neighbours(src, t, phases, count, lo, hi, wanted):
        i = t * phases + p
        ee = e[i, lo:hi]
        found.append(jnp.where(ee > 0.0, (g[i, lo:hi] + near) - ee * x, 0.0))
    return found


def column_residual(src, g, e, phases, count, lo, hi, tmp):
    wanted = everything(phases, count)
    for start in range(lo, hi, CHUNK):
        part = slice(start, min(start + CHUNK, hi))
        for t in wanted:
            r = residual_of(src, g, e, t, phases, count, part.start, part.stop, wanted[t])
            for k, p in enumerate(wanted[t][::2]):
                tmp[(t * phases + p) // 2, part] = r[2 * k] + r[2 * k + 1]


def rows_op(src, i, lo, rows, op):
    return op(src[i, pl.ds(lo, rows, stride=2)], src[i, pl.ds(lo + 1, rows, stride=2)])


def restrict(tmp, planes, tlo, out, active, olo, rows):
    for i in range(planes):
        out[i, olo:olo + rows] = jnp.where(
            active[i, olo:olo + rows] > 0.0, rows_op(tmp, i, tlo, rows, jnp.add), 0.0)


def coarsen(src, i, lo, rows, op):
    return op(rows_op(src, 2 * i, lo, rows, op), rows_op(src, 2 * i + 1, lo, rows, op))


def correct(coarse, fine, b, planes, clo, rows, lo, tmp):
    hi = lo + 2 * rows
    for i in range(planes):
        c = coarse[i, clo:clo + rows]
        tmp[i, pl.ds(lo, rows, stride=2)] = c
        tmp[i, pl.ds(lo + 1, rows, stride=2)] = c
    for i in range(2 * planes):
        fine[i, lo:hi] = fine[i, lo:hi] + jnp.where(b[i, lo:hi] > 0.0, tmp[i // 2, lo:hi], 0.0)


def pack(src, t, lo, rows, op):
    x = rows_op(src, 2 * t, lo, rows, op)
    lane = lanes_of(x)
    x = op(x, pltpu.roll(x, LANES - 1, 1))
    if 2 * t + 1 < T2:
        y = rows_op(src, 2 * t + 1, lo, rows, op)
        x = jnp.where((lane & 1) == 0, x, op(y, pltpu.roll(y, 1, 1)))
        index = jnp.where(lane < HALF, 2 * lane, 2 * lane - (LANES - 1))
    else:
        index = (2 * lane) & (LANES - 1)
    return gather(x, index)


def unpack(coarse, fine, b, clo, rows, lo, tmp):
    hi = lo + 2 * rows
    for t in range(T2):
        c = coarse[t // 2, clo:clo + rows]
        lane = lanes_of(c)
        if t == T2 - 1:
            index = (lane >> 1) + jnp.where(lane < HALF, 0, HALF)
        else:
            index = (lane >> 1) + HALF * (t % 2)
        c = gather(c, index)
        tmp[t, pl.ds(lo, rows, stride=2)] = c
        tmp[t, pl.ds(lo + 1, rows, stride=2)] = c
    for t in range(T2):
        fine[t, lo:hi] = fine[t, lo:hi] + jnp.where(b[t, lo:hi] > 0.0, tmp[t, lo:hi], 0.0)


def masked_inverse(x):
    return jnp.where(x > 0.0, OMEGA / jnp.where(x > 0.0, x, 1.0), 0.0)


def kernel(lon_count, lat_count, guide, screen, valid, tiles, out, res,
           gin, win, vin, fin, nat, pack0, land0, mid, s0, b0, e0, v0, w0, tmp, vg, bb, e1, u1, wa, b2, e2, gg, v2, u2, r2, b3, g3, v3, u3,
           xbb, xwa, rvg, in_sem, send_sem, recv_sem):
    lon = lax.axis_index("lon")
    lat = lax.axis_index("lat")
    v1, g1, b1 = vg.at[0], vg.at[1], bb.at[0]
    w2, a2 = wa.at[0], wa.at[1]
    n0, n1, n2, n3 = P0 * T0, P1 * T1, P2 * T2, P3 * T3

    def peer(d):
        return {"lat": lax.rem(lat + DIRS[d][0] + lat_count, lat_count),
                "lon": lax.rem(lon + DIRS[d][1] + lon_count, lon_count)}

    def exists(dy):
        return lat > 0 if dy < 0 else lat < lat_count - 1 if dy > 0 else None

    def guarded(condition, fn):
        if condition is None:
            fn()
        else:
            pl.when(condition)(fn)

    barrier = pltpu.get_barrier_semaphore()
    for d in range(8):
        guarded(exists(DIRS[d][0]), lambda d=d: pl.semaphore_signal(
            barrier, inc=1, device_id=peer(d), device_id_type=MESH))

    loads = [pltpu.make_async_copy(src, dst, in_sem.at[i]) for i, (src, dst) in enumerate((
        (valid, vin), (screen, win), (guide, gin), (tiles, fin)))]
    for copy in loads:
        copy.start()

    for ref, lo, hi in ((v0, *A0), (w0, *A0), (v1, *A1), (u1, *A1), (v2, *A2), (u2, *A2), (v3, *A3), (u3, *A3)):
        zero = jnp.zeros((ref.shape[0], 8, LANES), jnp.float32)
        ref[:, lo - 8:lo] = zero
        ref[:, hi:hi + 8] = zero

    def copy_of(message, d):
        kind, parts = message
        src, dst = parts[d]
        return pltpu.make_async_remote_copy(
            src_ref=src, dst_ref=dst, send_sem=send_sem.at[kind, d], recv_sem=recv_sem.at[kind, d],
            device_id=peer(d), device_id_type=MESH)

    def send(message):
        for d in message[1]:
            guarded(exists(DIRS[d][0]), lambda d=d: copy_of(message, d).start())

    def sent(message):
        for d in message[1]:
            guarded(exists(DIRS[d][0]), lambda d=d: copy_of(message, d).wait_send())

    def received(message):
        for d in message[1]:
            guarded(exists(-DIRS[d][0]), lambda d=d: copy_of(message, d).wait_recv())

    def clear(refs, above, below):
        for edge, rows in ((lat == 0, above), (lat == lat_count - 1, below)):
            @pl.when(edge)
            def _():
                for ref in refs:
                    zero = jnp.zeros((rows[1] - rows[0], LANES), jnp.float32)
                    for i in range(ref.shape[0]):
                        ref[i, rows[0]:rows[1]] = zero

    def row_spans(dy, first, rows, depth, skip=0):
        if dy < 0:
            return pl.ds(first + skip, depth), pl.ds(first + rows + skip, depth)
        if dy > 0:
            return pl.ds(first + rows - depth - skip, depth), pl.ds(first - depth - skip, depth)
        return (pl.ds(first, rows),) * 2

    near_parts, far_parts, side_parts = {}, {}, {}
    for d, (dy, dx) in enumerate(DIRS):
        if dx == 0:
            for parts, skip in ((near_parts, 0), (far_parts, 8)):
                a, b = row_spans(dy, H0, N0, 8, skip)
                parts[d] = nat.at[:, :, a], nat.at[:, :, b]
        else:
            a, b = row_spans(dy, H0, N0, H0)
            side = 0 if dx < 0 else 1
            side_parts[d] = pack0.at[side, :, a], land0.at[side, :, b]
    near_message, far_message, side_message = (0, near_parts), (1, far_parts), (0, side_parts)

    def coarse_parts(ref, land, phases, first, rows, depth):
        parts = {}
        for d, (dy, dx) in enumerate(DIRS):
            a, b = row_spans(dy, first, rows, depth)
            if dx == 0:
                own = pl.ds(0, 2 * phases)
                parts[d] = ref.at[:, own, a], ref.at[:, own, b]
            else:
                mine, side = (0, 1) if dx < 0 else (phases, 0)
                parts[d] = ref.at[:, pl.ds(mine, phases), a], land.at[side, :, :, b]
        return parts

    def row_parts(src, dst, first, rows, depth):
        parts = {}
        for d in range(2):
            a, b = row_spans(DIRS[d][0], first, rows, depth)
            parts[d] = src.at[..., a, :], dst.at[..., b, :]
        return parts

    def merge(land, k, ref, phases, lo, hi):
        for p in range(phases):
            left = land[0, k, p, lo:hi]
            ref[2 * phases + p, lo:hi] = jnp.where(lanes_of(left) < HALF, land[1, k, p, lo:hi], left)

    for copy in loads:
        copy.wait()
    for t in range(OWN):
        cols = slice(t * LANES, (t + 1) * LANES)
        active = vin[:, cols].astype(jnp.float32) * fin[0, t].astype(jnp.float32)
        nat[0, t, H0:H0 + N0] = active * gin[:, cols]
        nat[1, t, H0:H0 + N0] = active * OMEGA / (4.0 + win[:, cols])
    own = slice(H0, H0 + N0)
    for side, near, far in ((0, 0, 1), (1, OWN - 1, OWN - 2)):
        for k in range(2):
            pack0[side, k, own] = nat[k, near, own]
        source, weight = nat[0, far, own], pltpu.roll(nat[1, far, own], HALF, 1)
        low = lanes_of(source) < HALF
        pack0[side, 2, own] = jnp.where(low, source, weight) if side == 0 else jnp.where(low, weight, source)
    interior = jnp.logical_and(lat > 0, lat < lat_count - 1).astype(jnp.int32)
    pl.semaphore_wait(barrier, 5 + 3 * interior)
    send(side_message)
    send(near_message)
    send(far_message)

    def arrange(t, lo, hi):
        for k, ref in enumerate((s0, b0)):
            def store(p, part, x, ref=ref):
                ref[P0 * t + p, lo + O0 - H0 + part.start:lo + O0 - H0 + part.stop] = x

            def tile(j, part):
                rows = slice(lo + part.start, lo + part.stop)
                if t < 2:
                    return nat[k, 4 * t + j, rows]
                side = 0 if j < 2 else 1
                if j in (0, 3):
                    return land0[side, k, rows]
                x = land0[side, 2, rows]
                if k == 1:
                    x = pltpu.roll(x, HALF, 1)
                low = lanes_of(x) < HALF
                return jnp.where(low, x, 0.0) if side == 0 else jnp.where(low, 0.0, x)

            split_phases([functools.partial(tile, j) for j in range(4)], mid.at[k], hi - lo, store)

    def columns(t):
        return slice(t * LANES, (t + 1) * LANES)

    for t in range(2):
        arrange(t, H0, H0 + N0)

        def store_weight(p, part, x):
            w0[P0 * t + p, part.start + O0:part.stop + O0] = x

        split_phases([lambda part, j=j: win[part, columns(4 * t + j)] for j in range(4)], mid.at[0], N0, store_weight)
    own = slice(O0, O0 + N0)
    for i in range(2 * P0):
        on = b0[i, own] > 0.0
        e0[i, own] = jnp.where(on, 4.0 + w0[i, own], 0.0)
        v0[i, own] = jnp.where(on, 1.0, 0.0)

    own = slice(O1, O1 + N1)
    for i in range(2 * P1):
        active = coarsen(v0, i, O0, N1, jnp.maximum)
        weight = coarsen(w0, i, O0, N1, jnp.add)
        diag = 4.0 + weight
        b1[i, own] = active * OMEGA / diag
        v1[i, own] = active
        u1[i, own] = weight
    message1 = (2, coarse_parts(bb, xbb, P1, O1, N1, H1))
    send(message1)

    for i in range(2 * P2):
        w2[i, O2:O2 + N2] = coarsen(u1, i, O1, N2, jnp.add)
        a2[i, O2:O2 + N2] = coarsen(v1, i, O1, N2, jnp.maximum)
    message2 = (3, coarse_parts(wa, xwa, P2, O2, N2, H2))
    send(message2)

    clear((nat.at[0], nat.at[1], land0.at[0], land0.at[1]), (0, H0), (H0 + N0, 2 * H0 + N0))

    def inverse(t, lo, hi):
        for i in range(P0 * t, P0 * t + P0):
            e0[i, lo + 8:hi + 8] = masked_inverse(b0[i, lo + 8:hi + 8])

    received(near_message)
    for t in range(T0 - 1):
        for lo, hi in ((8, H0), (H0 + N0, H0 + N0 + 8)):
            arrange(t, lo, hi)
            inverse(t, lo, hi)

    own = range(2 * P0)
    sides = range(2 * P0, n0)
    before, after = {0: (1, 2, 3), 1: (0, 1, 2)}, {0: (0,), 1: (3,), 2: (0, 1, 2, 3)}
    first_sweep(w0, s0, b0, own, *B0)
    sweep(w0, v0, s0, b0, P0, T0, *B0, before)

    received(side_message)
    arrange(T0 - 1, 0, 2 * H0 + N0)
    inverse(T0 - 1, 0, 2 * H0 + N0)
    first_sweep(w0, s0, b0, sides, *B0)
    sweep(w0, v0, s0, b0, P0, T0, *B0, after)
    column_residual(v0, s0, e0, P0, T0, *B0, tmp)

    for cycle in range(2):
        rows0 = A0 if cycle == 0 else B0
        g2 = gg.at[cycle]
        if cycle == 1:
            sweep(v0, w0, s0, b0, P0, T0, *B0)
            sweep(w0, v0, s0, b0, P0, T0, *B0)
            column_residual(v0, s0, e0, P0, T0, *B0, tmp)

        if cycle == 0:
            received(message1)
            clear((bb.at[0], xbb.at[0, 0], xbb.at[1, 0]), (O1 - H1, O1), (O1 + N1, O1 + N1 + H1))
            merge(xbb, 0, b1, P1, *A1)
            for i in range(n1):
                e1[i, A1[0]:A1[1]] = masked_inverse(b1[i, A1[0]:A1[1]])
        restrict(tmp, n1, A0[0], g1, b1, A1[0], A1[1] - A1[0])
        first_sweep(u1, g1, b1, range(n1), *A1)
        sweep(u1, v1, g1, b1, P1, T1, *A1)
        if cycle == 0:
            received(message2)
            clear((w2, a2, xwa.at[0, 0], xwa.at[0, 1], xwa.at[1, 0], xwa.at[1, 1]),
                  (O2 - H2, O2), (O2 + N2, O2 + N2 + H2))
            for k in range(2):
                merge(xwa, k, wa.at[k], P2, *A2)
        column_residual(v1, g1, e1, P1, T1, O1, O1 + N1, tmp)
        restrict(tmp, n2, O1, g2, a2, O2, N2)
        message_g = (4 + cycle, row_parts(g2, g2, O2, N2, H2))
        message_v = (6 + cycle, row_parts(vg, rvg.at[cycle], O1, N1, H1))
        send(message_g)
        send(message_v)

        if cycle == 0:
            received(far_message)
            for lo, hi in ((0, 8), (H0 + N0 + 8, 2 * H0 + N0)):
                for t in range(T0 - 1):
                    arrange(t, lo, hi)
                first_sweep(w0, s0, b0, range(n0), lo + 8, hi + 8)
            for lo, hi in ((A0[0], A0[0] + 16), (A0[1] - 16, A0[1])):
                sweep(w0, v0, s0, b0, P0, T0, lo, hi)
            lo, hi = A2
            for t in range(n2):
                diag = 4.0 + w2[t, lo:hi]
                b2[t, lo:hi] = a2[t, lo:hi] * OMEGA / diag
                e2[t, lo:hi] = a2[t, lo:hi] * diag
            lo, hi = A3
            for t in range(n3):
                b3[t, lo:hi] = pack(a2, t, A2[0], hi - lo, jnp.maximum) * OMEGA / (
                    4.0 + pack(w2, t, A2[0], hi - lo, jnp.add))
        received(message_g)
        clear((g2,), (O2 - H2, O2), (O2 + N2, O2 + N2 + H2))
        first_sweep(u2, g2, b2, range(n2), *A2)
        sweep(u2, v2, g2, b2, P2, T2, *A2)
        for t in range(n2):
            r2[t, A2[0]:A2[1]] = residual_of(v2, g2, e2, t, P2, T2, *A2, (0,))[0]
        lo, hi = A3
        for t in range(n3):
            g3[t, lo:hi] = jnp.where(b3[t, lo:hi] > 0.0, pack(r2, t, A2[0], hi - lo, jnp.add), 0.0)
        first_sweep(v3, g3, b3, range(n3), *A3)
        for i in range(7):
            src, dst = (v3, u3) if i % 2 == 0 else (u3, v3)
            sweep(src, dst, g3, b3, P3, T3, *A3)
        unpack(u3, v2, b2, A3[0], hi - lo, A2[0], tmp)
        sweep(v2, u2, g2, b2, P2, T2, *A2)
        sweep(u2, v2, g2, b2, P2, T2, *A2)

        sent(message_g)
        sent(message_v)
        received(message_v)
        clear((rvg.at[cycle, 0], rvg.at[cycle, 1]), (O1 - H1, O1), (O1 + N1, O1 + N1 + H1))
        for k in range(2):
            for i in range(n1):
                for lo, hi in ((A1[0], O1), (O1 + N1, A1[1])):
                    vg[k, i, lo:hi] = rvg[cycle, k, i, lo:hi]
        correct(v2, v1, b1, n2, O2 - 4, (A1[1] - A1[0]) // 2, A1[0], tmp)
        sweep(v1, u1, g1, b1, P1, T1, *A1)
        sweep(u1, v1, g1, b1, P1, T1, *A1)
        correct(v1, v0, b0, n1, A1[0], A1[1] - A1[0], A0[0], tmp)
        sweep(v0, w0, s0, b0, P0, T0, *rows0)
        sweep(w0, v0, s0, b0, P0, T0, *rows0)

    for k, stage in enumerate((out, res)):
        if k == 1:
            for t in range(2):
                for p, r in enumerate(residual_of(v0, s0, e0, t, P0, T0, O0, O0 + N0, tuple(range(P0)))):
                    w0[P0 * t + p, O0:O0 + N0] = r
        src = w0 if k == 1 else v0
        for t in range(2):
            def store_tile(j, x):
                stage[:, columns(4 * t + j)] = x

            join_phases([lambda part, p=p: src[P0 * t + p, part.start + O0:part.stop + O0] for p in range(P0)],
                        mid.at[t], N0, [functools.partial(store_tile, j) for j in range(4)])
    for message in (side_message, near_message, far_message, message1, message2):
        sent(message)


def store(a, b, out, res, sem):
    copies = [pltpu.make_async_copy(x, y, sem.at[i]) for i, (x, y) in enumerate(((a, out), (b, res)))]
    for copy in copies:
        copy.start()
    for copy in copies:
        copy.wait()


def solution(mesh):
    def body(guide, screen, valid, tiles):
        def vmem(*shape):
            return pltpu.VMEM(shape + (LANES,), jnp.float32)

        n0, n1, n2, n3 = P0 * T0, P1 * T1, P2 * T2, P3 * T3
        block = guide.shape
        guide, screen, valid, tiles = [
            pltpu.with_memory_space_constraint(x, pltpu.HBM) for x in (guide, screen, valid, tiles)]
        pair = pl.pallas_call(
            functools.partial(kernel, mesh.shape["lon"], mesh.shape["lat"]),
            out_shape=(pltpu.VMEM(block, jnp.float32),) * 2,
            in_specs=[pl.BlockSpec(memory_space=pl.ANY)] * 4,
            out_specs=(pl.BlockSpec(memory_space=pltpu.VMEM),) * 2,
            scratch_shapes=[
                pltpu.VMEM(block, jnp.float32), pltpu.VMEM(block, jnp.float32), pltpu.VMEM(block, jnp.int32),
                pltpu.SMEM((1, OWN), jnp.int32),
                vmem(2, OWN, N0 + 2 * H0), vmem(2, 3, N0 + 2 * H0), vmem(2, 3, N0 + 2 * H0), vmem(2, 4, N0 + 2 * H0), vmem(n0, R0), vmem(n0, R0), vmem(n0, R0), vmem(n0, R0), vmem(n0, R0),
                vmem(n1, R0),
                vmem(2, n1, R1), vmem(1, n1, R1), vmem(n1, R1), vmem(n1, R1),
                vmem(2, n2, R2), vmem(n2, R2), vmem(n2, R2), vmem(2, n2, R2), vmem(n2, R2), vmem(n2, R2), vmem(n2, R2),
                vmem(n3, R3), vmem(n3, R3), vmem(n3, R3), vmem(n3, R3),
                vmem(2, 1, P1, R1), vmem(2, 2, P2, R2), vmem(2, 2, n1, R1),
                pltpu.SemaphoreType.DMA((4,)), pltpu.SemaphoreType.DMA((8, 8)),
                pltpu.SemaphoreType.DMA((8, 8)),
            ],
            compiler_params=pltpu.CompilerParams(
                collective_id=0, has_side_effects=True, vmem_limit_bytes=48 * 1024 * 1024),
        )(guide, screen, valid, tiles)
        pair = [pltpu.with_memory_space_constraint(x, pltpu.VMEM) for x in pair]
        return pl.pallas_call(
            store,
            out_shape=(pltpu.HBM(block, jnp.float32),) * 2,
            in_specs=[pl.BlockSpec(memory_space=pl.ANY)] * 2,
            out_specs=(pl.BlockSpec(memory_space=pltpu.HBM),) * 2,
            scratch_shapes=[pltpu.SemaphoreType.DMA((2,))],
        )(*pair)

    spec = P("lat", "lon")
    return jax.shard_map(
        body, mesh=mesh, in_specs=(spec,) * 4, out_specs=(spec,) * 2, check_vma=False)
```

```python
import functools

import jax
import jax.numpy as jnp
from jax import lax
from jax.experimental import pallas as pl
from jax.experimental.pallas import tpu as pltpu
from jax.sharding import PartitionSpec as P

OMEGA = 0.8
MESH = pl.DeviceIdType.MESH
LANES = 128
CHUNK = 24
HALF = LANES // 2

P0, P1, P2, P3 = 4, 2, 1, 1
T0, T1, T2, T3 = 3, 3, 3, 2
O0, O1, O2, O3 = 24, 16, 32, 20
N0, N1, N2, N3 = 128, 64, 32, 16
R0, R1, R2, R3 = 176, 96, 96, 56
A0, B0, A1, A2, B2, A3 = (8, 168), (16, 160), (8, 88), (8, 88), (24, 72), (8, 48)
H0, H1, H2 = 16, 8, 24
OWN = 8
DIRS = ((-1, 0), (1, 0), (0, -1), (0, 1), (-1, -1), (-1, 1), (1, -1), (1, 1))


def lanes_of(x):
    return lax.broadcasted_iota(jnp.int32, x.shape, 1)


def gather(x, index):
    return jnp.take_along_axis(x, index, axis=1, mode="promise_in_bounds")


def barrel(tiles, lane):
    odd, high = (lane & 32) != 0, lane >= HALF
    half = [jnp.where(odd, tiles[(i + 1) % 4], tiles[i]) for i in range(4)]
    return [jnp.where(high, half[(i + 2) % 4], half[i]) for i in range(4)]


def group_phases(x, t):
    lane = lanes_of(x)
    return gather(x, ((lane & 31) << 2) + (((lane >> 5) + (4 - t)) & 3))


def split_phases(sources, rows, store):
    step = min(rows, 16)
    for row in range(0, rows, step):
        part = slice(row, row + step)
        tiles = [src(part) for src in sources]
        mixed = barrel(tiles, lanes_of(tiles[0]))
        store(0, part, mixed[0])
        for p in range(1, 4):
            store(p, part, pltpu.roll(mixed[4 - p], LANES - 32 * p, 1))


def join_phases(sources, mid, rows, stores):
    for row in range(0, rows, 16):
        part = slice(row, row + 16)
        phases = [src(part) for src in sources]
        placed = [phases[0]] + [pltpu.roll(phases[p], 32 * p, 1) for p in range(1, 4)]
        mixed = barrel(placed, lanes_of(placed[0]))
        for t in range(4):
            mid[t, part] = mixed[(4 - t) % 4]
    for t, store in enumerate(stores):
        x = mid[t, 0:rows]
        lane = lanes_of(x)
        store(gather(x, (((lane + t) & 3) << 5) + (lane >> 2)))


def neighbours(src, g, t, phases, count, lo, hi, wanted):
    base, last = t * phases, phases - 1
    row = [src[base + p, lo:hi] for p in range(phases)]
    lane = lanes_of(row[0])
    left = right = None
    if 0 in wanted:
        left = pltpu.roll(jnp.where(lane == LANES - 1, src[((t - 1) % count) * phases + last, lo:hi], row[last]), 1, 1)
    if last in wanted:
        right = pltpu.roll(jnp.where(lane == 0, src[((t + 1) % count) * phases, lo:hi], row[0]), LANES - 1, 1)
    row = [left] + row + [right]
    return [(p, row[p + 1], (g[base + p, lo:hi] + (src[base + p, lo - 1:hi - 1] + src[base + p, lo + 1:hi + 1])) + (
        row[p] + row[p + 2])) for p in wanted]


def everything(phases, count):
    return {t: tuple(range(phases)) for t in range(count)}


def sweep(src, dst, g, b, phases, count, lo, hi, wanted=None):
    wanted = wanted or everything(phases, count)
    for start in range(lo, hi, CHUNK):
        part = slice(start, min(start + CHUNK, hi))
        for t in wanted:
            for p, x, near in neighbours(src, g, t, phases, count, part.start, part.stop, wanted[t]):
                i = t * phases + p
                dst[i, part] = (1.0 - OMEGA) * x + b[i, part] * near


def first_sweep(dst, g, b, planes, lo, hi):
    for i in planes:
        dst[i, lo:hi] = b[i, lo:hi] * g[i, lo:hi]


def residual_of(src, g, e, t, phases, count, lo, hi, wanted):
    found = []
    for p, x, near in neighbours(src, g, t, phases, count, lo, hi, wanted):
        i = t * phases + p
        ee = e[i, lo:hi]
        found.append(jnp.where(ee > 0.0, near - ee * x, 0.0))
    return found


def column_residual(src, g, e, phases, count, lo, hi, tmp):
    wanted = everything(phases, count)
    for start in range(lo, hi, CHUNK):
        part = slice(start, min(start + CHUNK, hi))
        for t in wanted:
            r = residual_of(src, g, e, t, phases, count, part.start, part.stop, wanted[t])
            for k, p in enumerate(wanted[t][::2]):
                tmp[(t * phases + p) // 2, part] = r[2 * k] + r[2 * k + 1]


def rows_op(src, i, lo, rows, op):
    return op(src[i, pl.ds(lo, rows, stride=2)], src[i, pl.ds(lo + 1, rows, stride=2)])


def restrict(tmp, planes, tlo, out, active, olo, rows):
    for i in range(planes):
        out[i, olo:olo + rows] = jnp.where(
            active[i, olo:olo + rows] > 0.0, rows_op(tmp, i, tlo, rows, jnp.add), 0.0)


def coarsen(src, i, lo, rows, op):
    return op(rows_op(src, 2 * i, lo, rows, op), rows_op(src, 2 * i + 1, lo, rows, op))


def correct(coarse, fine, b, planes, clo, rows, lo, tmp):
    hi = lo + 2 * rows
    for i in range(planes):
        c = coarse[i, clo:clo + rows]
        tmp[i, pl.ds(lo, rows, stride=2)] = c
        tmp[i, pl.ds(lo + 1, rows, stride=2)] = c
    for i in range(2 * planes):
        fine[i, lo:hi] = fine[i, lo:hi] + jnp.where(b[i, lo:hi] > 0.0, tmp[i // 2, lo:hi], 0.0)


def pack(src, t, lo, rows, op):
    x = rows_op(src, 2 * t, lo, rows, op)
    lane = lanes_of(x)
    x = op(x, pltpu.roll(x, LANES - 1, 1))
    if 2 * t + 1 < T2:
        y = rows_op(src, 2 * t + 1, lo, rows, op)
        x = jnp.where((lane & 1) == 0, x, op(y, pltpu.roll(y, 1, 1)))
        index = jnp.where(lane < HALF, 2 * lane, 2 * lane - (LANES - 1))
    else:
        index = (2 * lane) & (LANES - 1)
    return gather(x, index)


def unpack(coarse, fine, b, clo, rows, lo, tmp):
    hi = lo + 2 * rows
    for t in range(T2):
        c = coarse[t // 2, clo:clo + rows]
        lane = lanes_of(c)
        if t == T2 - 1:
            index = (lane >> 1) + jnp.where(lane < HALF, 0, HALF)
        else:
            index = (lane >> 1) + HALF * (t % 2)
        c = gather(c, index)
        tmp[t, pl.ds(lo, rows, stride=2)] = c
        tmp[t, pl.ds(lo + 1, rows, stride=2)] = c
    for t in range(T2):
        fine[t, lo:hi] = fine[t, lo:hi] + jnp.where(b[t, lo:hi] > 0.0, tmp[t, lo:hi], 0.0)


def masked_inverse(x):
    return jnp.where(x > 0.0, OMEGA / jnp.where(x > 0.0, x, 1.0), 0.0)


def kernel(lon_count, lat_count, guide, screen, valid, tiles, out, res,
           gin, win, vin, fin, nat, pack0, land0, mid, s0, b0, e0, v0, w0, tmp, vg, bb, e1, u1, wa, b2, e2, gg, v2, u2, r2, b3, g3, v3, u3,
           xbb, xwa, rvg, in_sem, send_sem, recv_sem):
    lon = lax.axis_index("lon")
    lat = lax.axis_index("lat")
    v1, g1, b1 = vg.at[0], vg.at[1], bb.at[0]
    w2, a2 = wa.at[0], wa.at[1]
    n0, n1, n2, n3 = P0 * T0, P1 * T1, P2 * T2, P3 * T3

    def peer(d):
        return {"lat": lax.rem(lat + DIRS[d][0] + lat_count, lat_count),
                "lon": lax.rem(lon + DIRS[d][1] + lon_count, lon_count)}

    def exists(dy):
        return lat > 0 if dy < 0 else lat < lat_count - 1 if dy > 0 else None

    def guarded(condition, fn):
        if condition is None:
            fn()
        else:
            pl.when(condition)(fn)

    barrier = pltpu.get_barrier_semaphore()
    def by_row(directions, fn, sign=1):
        for dy in (-1, 1, 0):
            chosen = [d for d in directions if DIRS[d][0] == dy]

            def run(chosen=chosen):
                for d in chosen:
                    fn(d)

            if chosen:
                guarded(exists(sign * dy), run)

    by_row(range(8), lambda d: pl.semaphore_signal(barrier, inc=1, device_id=peer(d), device_id_type=MESH))

    outer, inner = (0, 1, OWN - 2, OWN - 1), tuple(range(2, OWN - 2))
    flag_copy = pltpu.make_async_copy(tiles, fin, in_sem.at[3, 0])
    loads = [[pltpu.make_async_copy(src.at[:, cols], dst.at[:, cols], in_sem.at[i, k])
              for i, (src, dst) in enumerate(((valid, vin), (screen, win), (guide, gin)))]
             for k, cols in enumerate((pl.ds(0, 2 * LANES), pl.ds((OWN - 2) * LANES, 2 * LANES),
                                       pl.ds(2 * LANES, (OWN - 4) * LANES)))]
    flag_copy.start()
    for part in loads:
        for copy in part:
            copy.start()

    for ref, lo, hi in ((v0, *A0), (w0, *A0), (v1, *A1), (u1, *A1), (v2, *A2), (u2, *A2), (v3, *A3), (u3, *A3)):
        zero = jnp.zeros((ref.shape[0], 8, LANES), jnp.float32)
        ref[:, lo - 8:lo] = zero
        ref[:, hi:hi + 8] = zero

    def copy_of(message, d):
        kind, parts = message
        src, dst = parts[d]
        return pltpu.make_async_remote_copy(
            src_ref=src, dst_ref=dst, send_sem=send_sem.at[kind, d], recv_sem=recv_sem.at[kind, d],
            device_id=peer(d), device_id_type=MESH)

    def send(message):
        by_row(message[1], lambda d: copy_of(message, d).start())

    def sent(message):
        by_row(message[1], lambda d: copy_of(message, d).wait_send())

    def received(message):
        by_row(message[1], lambda d: copy_of(message, d).wait_recv(), -1)

    def clear(refs, above, below):
        for edge, rows in ((lat == 0, above), (lat == lat_count - 1, below)):
            @pl.when(edge)
            def _():
                for ref in refs:
                    zero = jnp.zeros((rows[1] - rows[0], LANES), jnp.float32)
                    for i in range(ref.shape[0]):
                        ref[i, rows[0]:rows[1]] = zero

    def row_spans(dy, first, rows, depth, skip=0):
        if dy < 0:
            return pl.ds(first + skip, depth), pl.ds(first + rows + skip, depth)
        if dy > 0:
            return pl.ds(first + rows - depth - skip, depth), pl.ds(first - depth - skip, depth)
        return (pl.ds(first, rows),) * 2

    near_parts, far_parts, side_parts = {}, {}, {}
    for d, (dy, dx) in enumerate(DIRS):
        if dx == 0:
            for parts, skip in ((near_parts, 0), (far_parts, 8)):
                a, b = row_spans(dy, H0, N0, 8, skip)
                parts[d] = nat.at[:, :, a], nat.at[:, :, b]
        else:
            a, b = row_spans(dy, H0, N0, H0)
            side = 0 if dx < 0 else 1
            side_parts[d] = pack0.at[side, :, a], land0.at[side, :, b]
    near_message, far_message, side_message = (0, near_parts), (1, far_parts), (0, side_parts)

    def coarse_parts(ref, land, phases, first, rows, depth):
        parts = {}
        for d, (dy, dx) in enumerate(DIRS):
            a, b = row_spans(dy, first, rows, depth)
            if dx == 0:
                own = pl.ds(0, 2 * phases)
                parts[d] = ref.at[:, own, a], ref.at[:, own, b]
            else:
                mine, side = (0, 1) if dx < 0 else (phases, 0)
                parts[d] = ref.at[:, pl.ds(mine, phases), a], land.at[side, :, :, b]
        return parts

    def row_parts(src, dst, first, rows, depth):
        parts = {}
        for d in range(2):
            a, b = row_spans(DIRS[d][0], first, rows, depth)
            parts[d] = src.at[..., a, :], dst.at[..., b, :]
        return parts

    def merge(land, k, ref, phases, lo, hi):
        for p in range(phases):
            left = land[0, k, p, lo:hi]
            ref[2 * phases + p, lo:hi] = jnp.where(lanes_of(left) < HALF, land[1, k, p, lo:hi], left)

    def prepare(t):
        cols = slice(t * LANES, (t + 1) * LANES)
        active = vin[:, cols].astype(jnp.float32) * fin[0, t].astype(jnp.float32)
        nat[0, t, H0:H0 + N0] = active * gin[:, cols]
        nat[1, t, H0:H0 + N0] = active * OMEGA / (4.0 + win[:, cols])

    flag_copy.wait()
    for copy in loads[0] + loads[1]:
        copy.wait()
    for t in outer:
        prepare(t)
    own = slice(H0, H0 + N0)
    for side, near, far in ((0, 0, 1), (1, OWN - 1, OWN - 2)):
        for k in range(2):
            pack0[side, k, own] = group_phases(nat[k, near, own], near % 4)
        source, weight = group_phases(nat[0, far, own], far % 4), group_phases(nat[1, far, own], far % 4)
        low = (lanes_of(source) & 16) == 0
        if side == 0:
            pack0[side, 2, own] = jnp.where(low, source, pltpu.roll(weight, 16, 1))
        else:
            pack0[side, 2, own] = jnp.where(low, pltpu.roll(weight, LANES - 16, 1), source)
    interior = jnp.logical_and(lat > 0, lat < lat_count - 1).astype(jnp.int32)
    pl.semaphore_wait(barrier, 5 + 3 * interior)
    send(side_message)
    for copy in loads[2]:
        copy.wait()
    for t in inner:
        prepare(t)
    send(near_message)
    send(far_message)

    def arrange(t, lo, hi, arrays=(0, 1)):
        for k in arrays:
            ref = (s0, b0)[k]

            def store(p, part, x, ref=ref):
                ref[P0 * t + p, lo + O0 - H0 + part.start:lo + O0 - H0 + part.stop] = x

            def tile(j, part):
                if t < 2:
                    return mid[k, j, part]
                rows = slice(lo + part.start, lo + part.stop)
                side = 0 if j < 2 else 1
                if j in (0, 3):
                    return land0[side, k, rows]
                x = land0[side, 2, rows]
                if k == 1:
                    x = pltpu.roll(x, LANES - 16 if side == 0 else 16, 1)
                low = (lanes_of(x) & 16) == 0
                return jnp.where(low, x, 0.0) if side == 0 else jnp.where(low, 0.0, x)

            if t < 2:
                for j in range(4):
                    mid[k, j, 0:hi - lo] = group_phases(nat[k, 4 * t + j, lo:hi], j)
            split_phases([functools.partial(tile, j) for j in range(4)], hi - lo, store)

    def columns(t):
        return slice(t * LANES, (t + 1) * LANES)

    for t in range(2):
        arrange(t, H0, H0 + N0, (1,))

        def store_weight(p, part, x):
            w0[P0 * t + p, part.start + O0:part.stop + O0] = x

        for j in range(4):
            mid[0, j, 0:N0] = group_phases(win[:, columns(4 * t + j)], j)
        split_phases([lambda part, j=j: mid[0, j, part] for j in range(4)], N0, store_weight)
    own = slice(O0, O0 + N0)
    for i in range(2 * P0):
        v0[i, own] = jnp.where(b0[i, own] > 0.0, 1.0, 0.0)

    own = slice(O1, O1 + N1)
    for i in range(2 * P1):
        active = coarsen(v0, i, O0, N1, jnp.maximum)
        weight = coarsen(w0, i, O0, N1, jnp.add)
        diag = 4.0 + weight
        b1[i, own] = active * OMEGA / diag
        v1[i, own] = active
        u1[i, own] = weight
    message1 = (2, coarse_parts(bb, xbb, P1, O1, N1, H1))
    send(message1)

    for i in range(2 * P2):
        w2[i, O2:O2 + N2] = coarsen(u1, i, O1, N2, jnp.add)
        a2[i, O2:O2 + N2] = coarsen(v1, i, O1, N2, jnp.maximum)
    message2 = (3, coarse_parts(wa, xwa, P2, O2, N2, H2))
    send(message2)

    own = slice(O0, O0 + N0)
    for t in range(2):
        arrange(t, H0, H0 + N0, (0,))
    for i in range(2 * P0):
        e0[i, own] = jnp.where(b0[i, own] > 0.0, 4.0 + w0[i, own], 0.0)

    clear((nat.at[0], nat.at[1], land0.at[0], land0.at[1]), (0, H0), (H0 + N0, 2 * H0 + N0))

    def inverse(t, lo, hi):
        for i in range(P0 * t, P0 * t + P0):
            e0[i, lo + 8:hi + 8] = masked_inverse(b0[i, lo + 8:hi + 8])

    received(near_message)
    for t in range(T0 - 1):
        for lo, hi in ((8, H0), (H0 + N0, H0 + N0 + 8)):
            arrange(t, lo, hi)
            inverse(t, lo, hi)

    own = range(2 * P0)
    sides = range(2 * P0, n0)
    before, after = {0: (1, 2, 3), 1: (0, 1, 2)}, {0: (0,), 1: (3,), 2: (0, 1, 2, 3)}
    first_sweep(w0, s0, b0, own, *B0)
    sweep(w0, v0, s0, b0, P0, T0, *B0, before)

    received(side_message)
    arrange(T0 - 1, 0, 2 * H0 + N0)
    inverse(T0 - 1, 0, 2 * H0 + N0)
    first_sweep(w0, s0, b0, sides, *B0)
    sweep(w0, v0, s0, b0, P0, T0, *B0, after)
    column_residual(v0, s0, e0, P0, T0, *B0, tmp)

    for cycle in range(2):
        rows0 = A0 if cycle == 0 else B0
        g2 = gg.at[cycle]
        if cycle == 1:
            sweep(v0, w0, s0, b0, P0, T0, *B0)
            sweep(w0, v0, s0, b0, P0, T0, *B0)
            column_residual(v0, s0, e0, P0, T0, *B0, tmp)

        if cycle == 0:
            received(message1)
            clear((bb.at[0], xbb.at[0, 0], xbb.at[1, 0]), (O1 - H1, O1), (O1 + N1, O1 + N1 + H1))
            merge(xbb, 0, b1, P1, *A1)
            for i in range(n1):
                e1[i, A1[0]:A1[1]] = masked_inverse(b1[i, A1[0]:A1[1]])
        restrict(tmp, n1, A0[0], g1, b1, A1[0], A1[1] - A1[0])
        first_sweep(u1, g1, b1, range(n1), *A1)
        sweep(u1, v1, g1, b1, P1, T1, *A1)
        column_residual(v1, g1, e1, P1, T1, O1, O1 + N1, tmp)
        for t in range(n2):
            on = coarsen(b1, t, O1, N2, jnp.maximum) > 0.0
            g2[t, O2:O2 + N2] = jnp.where(on, rows_op(tmp, t, O1, N2, jnp.add), 0.0)
        message_g = (4 + cycle, row_parts(g2, g2, O2, N2, H2))
        message_v = (6 + cycle, row_parts(vg, rvg.at[cycle], O1, N1, H1))
        send(message_g)
        send(message_v)

        if cycle == 0:
            received(far_message)
            for lo, hi in ((0, 8), (H0 + N0 + 8, 2 * H0 + N0)):
                for t in range(T0 - 1):
                    arrange(t, lo, hi)
                first_sweep(w0, s0, b0, range(n0), lo + 8, hi + 8)
            for lo, hi in ((A0[0], A0[0] + 16), (A0[1] - 16, A0[1])):
                sweep(w0, v0, s0, b0, P0, T0, lo, hi)
            received(message2)
            clear((w2, a2, xwa.at[0, 0], xwa.at[0, 1], xwa.at[1, 0], xwa.at[1, 1]),
                  (O2 - H2, O2), (O2 + N2, O2 + N2 + H2))
            for k in range(2):
                merge(xwa, k, wa.at[k], P2, *A2)
            lo, hi = A2
            for t in range(n2):
                diag = 4.0 + w2[t, lo:hi]
                b2[t, lo:hi] = a2[t, lo:hi] * OMEGA / diag
                e2[t, lo:hi] = a2[t, lo:hi] * diag
            lo, hi = A3
            for t in range(n3):
                b3[t, lo:hi] = pack(a2, t, A2[0], hi - lo, jnp.maximum) * OMEGA / (
                    4.0 + pack(w2, t, A2[0], hi - lo, jnp.add))
        received(message_g)
        clear((g2,), (O2 - H2, O2), (O2 + N2, O2 + N2 + H2))
        first_sweep(u2, g2, b2, range(n2), *A2)
        sweep(u2, v2, g2, b2, P2, T2, *A2)
        for t in range(n2):
            r2[t, A2[0]:A2[1]] = residual_of(v2, g2, e2, t, P2, T2, *A2, (0,))[0]
        lo, hi = A3
        for t in range(n3):
            g3[t, lo:hi] = jnp.where(b3[t, lo:hi] > 0.0, pack(r2, t, A2[0], hi - lo, jnp.add), 0.0)
        first_sweep(v3, g3, b3, range(n3), *A3)
        for i in range(7):
            src, dst = (v3, u3) if i % 2 == 0 else (u3, v3)
            sweep(src, dst, g3, b3, P3, T3, *A3)
        unpack(u3, v2, b2, A3[0] + (B2[0] - A2[0]) // 2, (B2[1] - B2[0]) // 2, B2[0], tmp)
        sweep(v2, u2, g2, b2, P2, T2, *B2)
        sweep(u2, v2, g2, b2, P2, T2, *B2)

        sent(message_g)
        sent(message_v)
        received(message_v)
        clear((rvg.at[cycle, 0], rvg.at[cycle, 1]), (O1 - H1, O1), (O1 + N1, O1 + N1 + H1))
        for k in range(2):
            for i in range(n1):
                for lo, hi in ((A1[0], O1), (O1 + N1, A1[1])):
                    vg[k, i, lo:hi] = rvg[cycle, k, i, lo:hi]
        correct(v2, v1, b1, n2, O2 - 4, (A1[1] - A1[0]) // 2, A1[0], tmp)
        sweep(v1, u1, g1, b1, P1, T1, *A1)
        sweep(u1, v1, g1, b1, P1, T1, *A1)
        correct(v1, v0, b0, n1, A1[0], A1[1] - A1[0], A0[0], tmp)
        sweep(v0, w0, s0, b0, P0, T0, *rows0)
        sweep(w0, v0, s0, b0, P0, T0, *rows0)

    own = slice(O0, O0 + N0)
    for t in range(2):
        for p, r in enumerate(residual_of(v0, s0, e0, t, P0, T0, own.start, own.stop, tuple(range(P0)))):
            i = P0 * t + p
            out[i] = v0[i, own]
            res[i] = r
    for message in (side_message, near_message, far_message, message1, message2):
        sent(message)


def store(a, b, out, res, stage, mid, sem):
    copies = []
    for k, (src, dst) in enumerate(((a, out), (b, res))):
        for t in range(2):
            def store_tile(j, x):
                stage[k, :, (4 * t + j) * LANES:(4 * t + j + 1) * LANES] = x

            join_phases([lambda part, p=p: src[P0 * t + p, part] for p in range(P0)], mid, N0,
                        [functools.partial(store_tile, j) for j in range(4)])
            half = pl.ds(4 * t * LANES, 4 * LANES)
            copies.append(pltpu.make_async_copy(stage.at[k, :, half], dst.at[:, half], sem.at[k, t]))
            copies[-1].start()
    for copy in copies:
        copy.wait()


def solution(mesh):
    def body(guide, screen, valid, tiles):
        def vmem(*shape):
            return pltpu.VMEM(shape + (LANES,), jnp.float32)

        n0, n1, n2, n3 = P0 * T0, P1 * T1, P2 * T2, P3 * T3
        block = guide.shape
        guide, screen, valid, tiles = [
            pltpu.with_memory_space_constraint(x, pltpu.HBM) for x in (guide, screen, valid, tiles)]
        pair = pl.pallas_call(
            functools.partial(kernel, mesh.shape["lon"], mesh.shape["lat"]),
            out_shape=(pltpu.VMEM((2 * P0, N0, LANES), jnp.float32),) * 2,
            in_specs=[pl.BlockSpec(memory_space=pl.ANY)] * 4,
            out_specs=(pl.BlockSpec(memory_space=pltpu.VMEM),) * 2,
            scratch_shapes=[
                pltpu.VMEM(block, jnp.float32), pltpu.VMEM(block, jnp.float32), pltpu.VMEM(block, jnp.int32),
                pltpu.SMEM((1, OWN), jnp.int32),
                vmem(2, OWN, N0 + 2 * H0), vmem(2, 3, N0 + 2 * H0), vmem(2, 3, N0 + 2 * H0), vmem(2, 4, N0 + 2 * H0), vmem(n0, R0), vmem(n0, R0), vmem(n0, R0), vmem(n0, R0), vmem(n0, R0),
                vmem(n1, R0),
                vmem(2, n1, R1), vmem(1, n1, R1), vmem(n1, R1), vmem(n1, R1),
                vmem(2, n2, R2), vmem(n2, R2), vmem(n2, R2), vmem(2, n2, R2), vmem(n2, R2), vmem(n2, R2), vmem(n2, R2),
                vmem(n3, R3), vmem(n3, R3), vmem(n3, R3), vmem(n3, R3),
                vmem(2, 1, P1, R1), vmem(2, 2, P2, R2), vmem(2, 2, n1, R1),
                pltpu.SemaphoreType.DMA((4, 3)), pltpu.SemaphoreType.DMA((8, 8)),
                pltpu.SemaphoreType.DMA((8, 8)),
            ],
            compiler_params=pltpu.CompilerParams(
                collective_id=0, has_side_effects=True, vmem_limit_bytes=48 * 1024 * 1024),
        )(guide, screen, valid, tiles)
        pair = [pltpu.with_memory_space_constraint(x, pltpu.VMEM) for x in pair]
        return pl.pallas_call(
            store,
            out_shape=(pltpu.HBM(block, jnp.float32),) * 2,
            in_specs=[pl.BlockSpec(memory_space=pltpu.VMEM)] * 2,
            out_specs=(pl.BlockSpec(memory_space=pltpu.HBM),) * 2,
            scratch_shapes=[pltpu.VMEM((2,) + block, jnp.float32), vmem(4, N0), pltpu.SemaphoreType.DMA((2, 2))],
        )(*pair)

    spec = P("lat", "lon")
    return jax.shard_map(
        body, mesh=mesh, in_specs=(spec,) * 4, out_specs=(spec,) * 2, check_vma=False)
```

```python
import functools

import jax
import jax.numpy as jnp
from jax import lax
from jax.experimental import pallas as pl
from jax.experimental.pallas import tpu as pltpu
from jax.sharding import PartitionSpec as P

OMEGA = 0.8
MESH = pl.DeviceIdType.MESH
LANES = 128
CHUNK = 24
HALF = LANES // 2

P0, P1, P2, P3 = 4, 2, 1, 1
T0, T1, T2, T3 = 3, 3, 3, 2
O0, O1, O2, O3 = 24, 16, 32, 20
N0, N1, N2, N3 = 128, 64, 32, 16
R0, R1, R2, R3 = 176, 96, 96, 56
A0, B0, A1, A2, B2, A3 = (8, 168), (16, 160), (8, 88), (8, 88), (24, 72), (8, 48)
H0, H1, H2 = 16, 8, 24
OWN = 8
DIRS = ((-1, 0), (1, 0), (0, -1), (0, 1), (-1, -1), (-1, 1), (1, -1), (1, 1))


def lanes_of(x):
    return lax.broadcasted_iota(jnp.int32, x.shape, 1)


def gather(x, index):
    return jnp.take_along_axis(x, index, axis=1, mode="promise_in_bounds")


def barrel(tiles, lane):
    odd, high = (lane & 32) != 0, lane >= HALF
    half = [jnp.where(odd, tiles[(i + 1) % 4], tiles[i]) for i in range(4)]
    return [jnp.where(high, half[(i + 2) % 4], half[i]) for i in range(4)]


def group_phases(x, t):
    lane = lanes_of(x)
    return gather(x, ((lane & 31) << 2) + (((lane >> 5) + (4 - t)) & 3))


def split_phases(sources, rows, store):
    step = min(rows, 16)
    for row in range(0, rows, step):
        part = slice(row, row + step)
        tiles = [src(part) for src in sources]
        mixed = barrel(tiles, lanes_of(tiles[0]))
        store(0, part, mixed[0])
        for p in range(1, 4):
            store(p, part, pltpu.roll(mixed[4 - p], LANES - 32 * p, 1))


def join_phases(sources, mid, rows, stores):
    for row in range(0, rows, 16):
        part = slice(row, row + 16)
        phases = [src(part) for src in sources]
        placed = [phases[0]] + [pltpu.roll(phases[p], 32 * p, 1) for p in range(1, 4)]
        mixed = barrel(placed, lanes_of(placed[0]))
        for t in range(4):
            mid[t, part] = mixed[(4 - t) % 4]
    for t, store in enumerate(stores):
        x = mid[t, 0:rows]
        lane = lanes_of(x)
        store(gather(x, (((lane + t) & 3) << 5) + (lane >> 2)))


def neighbours(src, g, t, phases, count, lo, hi, wanted):
    base, last = t * phases, phases - 1
    row = [src[base + p, lo:hi] for p in range(phases)]
    lane = lanes_of(row[0])
    left = right = None
    if 0 in wanted:
        left = pltpu.roll(jnp.where(lane == LANES - 1, src[((t - 1) % count) * phases + last, lo:hi], row[last]), 1, 1)
    if last in wanted:
        right = pltpu.roll(jnp.where(lane == 0, src[((t + 1) % count) * phases, lo:hi], row[0]), LANES - 1, 1)
    row = [left] + row + [right]
    return [(p, row[p + 1], (g[base + p, lo:hi] + (src[base + p, lo - 1:hi - 1] + src[base + p, lo + 1:hi + 1])) + (
        row[p] + row[p + 2])) for p in wanted]


def everything(phases, count):
    return {t: tuple(range(phases)) for t in range(count)}


def sweep(src, dst, g, b, phases, count, lo, hi, wanted=None):
    wanted = wanted or everything(phases, count)
    for start in range(lo, hi, CHUNK):
        part = slice(start, min(start + CHUNK, hi))
        for t in wanted:
            for p, x, near in neighbours(src, g, t, phases, count, part.start, part.stop, wanted[t]):
                i = t * phases + p
                dst[i, part] = (1.0 - OMEGA) * x + b[i, part] * near


def first_sweep(dst, g, b, planes, lo, hi):
    for i in planes:
        dst[i, lo:hi] = b[i, lo:hi] * g[i, lo:hi]


def residual_of(src, g, e, t, phases, count, lo, hi, wanted):
    found = []
    for p, x, near in neighbours(src, g, t, phases, count, lo, hi, wanted):
        i = t * phases + p
        ee = e[i, lo:hi]
        found.append(jnp.where(ee > 0.0, near - ee * x, 0.0))
    return found


def column_residual(src, g, e, phases, count, lo, hi, tmp):
    wanted = everything(phases, count)
    for start in range(lo, hi, CHUNK):
        part = slice(start, min(start + CHUNK, hi))
        for t in wanted:
            r = residual_of(src, g, e, t, phases, count, part.start, part.stop, wanted[t])
            for k, p in enumerate(wanted[t][::2]):
                tmp[(t * phases + p) // 2, part] = r[2 * k] + r[2 * k + 1]


def rows_op(src, i, lo, rows, op):
    return op(src[i, pl.ds(lo, rows, stride=2)], src[i, pl.ds(lo + 1, rows, stride=2)])


def restrict(tmp, planes, tlo, out, active, olo, rows):
    for i in range(planes):
        out[i, olo:olo + rows] = jnp.where(
            active[i, olo:olo + rows] > 0.0, rows_op(tmp, i, tlo, rows, jnp.add), 0.0)


def coarsen(src, i, lo, rows, op):
    return op(rows_op(src, 2 * i, lo, rows, op), rows_op(src, 2 * i + 1, lo, rows, op))


def correct(coarse, fine, b, planes, clo, rows, lo, tmp):
    hi = lo + 2 * rows
    for i in range(planes):
        c = coarse[i, clo:clo + rows]
        tmp[i, pl.ds(lo, rows, stride=2)] = c
        tmp[i, pl.ds(lo + 1, rows, stride=2)] = c
    for i in range(2 * planes):
        fine[i, lo:hi] = fine[i, lo:hi] + jnp.where(b[i, lo:hi] > 0.0, tmp[i // 2, lo:hi], 0.0)


def pack(src, t, lo, rows, op):
    x = rows_op(src, 2 * t, lo, rows, op)
    lane = lanes_of(x)
    x = op(x, pltpu.roll(x, LANES - 1, 1))
    if 2 * t + 1 < T2:
        y = rows_op(src, 2 * t + 1, lo, rows, op)
        x = jnp.where((lane & 1) == 0, x, op(y, pltpu.roll(y, 1, 1)))
        index = jnp.where(lane < HALF, 2 * lane, 2 * lane - (LANES - 1))
    else:
        index = (2 * lane) & (LANES - 1)
    return gather(x, index)


def unpack(coarse, fine, b, clo, rows, lo, tmp):
    hi = lo + 2 * rows
    for t in range(T2):
        c = coarse[t // 2, clo:clo + rows]
        lane = lanes_of(c)
        if t == T2 - 1:
            index = (lane >> 1) + jnp.where(lane < HALF, 0, HALF)
        else:
            index = (lane >> 1) + HALF * (t % 2)
        c = gather(c, index)
        tmp[t, pl.ds(lo, rows, stride=2)] = c
        tmp[t, pl.ds(lo + 1, rows, stride=2)] = c
    for t in range(T2):
        fine[t, lo:hi] = fine[t, lo:hi] + jnp.where(b[t, lo:hi] > 0.0, tmp[t, lo:hi], 0.0)


def masked_inverse(x):
    return jnp.where(x > 0.0, OMEGA / jnp.where(x > 0.0, x, 1.0), 0.0)


def kernel(lon_count, lat_count, guide, screen, valid, tiles, out, res,
           gin, win, vin, fin, nat, pack0, land0, mid, s0, b0, e0, v0, w0, tmp, vg, bb, e1, u1, wa, b2, e2, gg, v2, u2, r2, b3, g3, v3, u3,
           xbb, xwa, rvg, in_sem, send_sem, recv_sem):
    lon = lax.axis_index("lon")
    lat = lax.axis_index("lat")
    v1, g1, b1 = vg.at[0], vg.at[1], bb.at[0]
    w2, a2 = wa.at[0], wa.at[1]
    n0, n1, n2, n3 = P0 * T0, P1 * T1, P2 * T2, P3 * T3

    def peer(d):
        return {"lat": lax.rem(lat + DIRS[d][0] + lat_count, lat_count),
                "lon": lax.rem(lon + DIRS[d][1] + lon_count, lon_count)}

    def exists(dy):
        return lat > 0 if dy < 0 else lat < lat_count - 1 if dy > 0 else None

    def guarded(condition, fn):
        if condition is None:
            fn()
        else:
            pl.when(condition)(fn)

    barrier = pltpu.get_barrier_semaphore()
    def by_row(directions, fn, sign=1):
        for dy in (-1, 1, 0):
            chosen = [d for d in directions if DIRS[d][0] == dy]

            def run(chosen=chosen):
                for d in chosen:
                    fn(d)

            if chosen:
                guarded(exists(sign * dy), run)

    by_row(range(8), lambda d: pl.semaphore_signal(barrier, inc=1, device_id=peer(d), device_id_type=MESH))

    outer, inner = (0, 1, OWN - 2, OWN - 1), tuple(range(2, OWN - 2))
    flag_copy = pltpu.make_async_copy(tiles, fin, in_sem.at[3, 0])
    loads = [[pltpu.make_async_copy(src.at[:, cols], dst.at[:, cols], in_sem.at[i, k])
              for i, (src, dst) in enumerate(((valid, vin), (screen, win), (guide, gin)))]
             for k, cols in enumerate((pl.ds(0, 2 * LANES), pl.ds((OWN - 2) * LANES, 2 * LANES),
                                       pl.ds(2 * LANES, (OWN - 4) * LANES)))]
    flag_copy.start()
    for part in loads:
        for copy in part:
            copy.start()

    for ref, lo, hi in ((v0, *A0), (w0, *A0), (v1, *A1), (u1, *A1), (v2, *A2), (u2, *A2), (v3, *A3), (u3, *A3)):
        zero = jnp.zeros((ref.shape[0], 8, LANES), jnp.float32)
        ref[:, lo - 8:lo] = zero
        ref[:, hi:hi + 8] = zero

    def copy_of(message, d):
        kind, parts = message
        src, dst = parts[d]
        return pltpu.make_async_remote_copy(
            src_ref=src, dst_ref=dst, send_sem=send_sem.at[kind, d], recv_sem=recv_sem.at[kind, d],
            device_id=peer(d), device_id_type=MESH)

    def send(message):
        by_row(message[1], lambda d: copy_of(message, d).start())

    def sent(message):
        by_row(message[1], lambda d: copy_of(message, d).wait_send())

    def received(message):
        by_row(message[1], lambda d: copy_of(message, d).wait_recv(), -1)

    def clear(refs, above, below):
        for edge, rows in ((lat == 0, above), (lat == lat_count - 1, below)):
            @pl.when(edge)
            def _():
                for ref in refs:
                    zero = jnp.zeros((rows[1] - rows[0], LANES), jnp.float32)
                    for i in range(ref.shape[0]):
                        ref[i, rows[0]:rows[1]] = zero

    def row_spans(dy, first, rows, depth, skip=0):
        if dy < 0:
            return pl.ds(first + skip, depth), pl.ds(first + rows + skip, depth)
        if dy > 0:
            return pl.ds(first + rows - depth - skip, depth), pl.ds(first - depth - skip, depth)
        return (pl.ds(first, rows),) * 2

    near_parts, far_parts, side_parts, late_parts = {}, {}, {}, {}
    for d, (dy, dx) in enumerate(DIRS):
        if dx == 0:
            for parts, skip in ((near_parts, 0), (far_parts, 8)):
                a, b = row_spans(dy, H0, N0, 8, skip)
                parts[d] = nat.at[:, :, a], nat.at[:, :, b]
        else:
            a, b = row_spans(dy, H0, N0, H0)
            side = 0 if dx < 0 else 1
            if dy == 0:
                a, late = (pl.ds(H0 + k * (N0 // 2), N0 // 2) for k in range(2))
                b = a
                late_parts[d] = pack0.at[side, :, late], land0.at[side, :, late]
            side_parts[d] = pack0.at[side, :, a], land0.at[side, :, b]
    near_message, far_message = (0, near_parts), (1, far_parts)
    side_message, late_message = (0, side_parts), (8, late_parts)

    def coarse_parts(ref, land, phases, first, rows, depth):
        parts = {}
        for d, (dy, dx) in enumerate(DIRS):
            a, b = row_spans(dy, first, rows, depth)
            if dx == 0:
                own = pl.ds(0, 2 * phases)
                parts[d] = ref.at[:, own, a], ref.at[:, own, b]
            else:
                mine, side = (0, 1) if dx < 0 else (phases, 0)
                parts[d] = ref.at[:, pl.ds(mine, phases), a], land.at[side, :, :, b]
        return parts

    def row_parts(src, dst, first, rows, depth):
        parts = {}
        for d in range(2):
            a, b = row_spans(DIRS[d][0], first, rows, depth)
            parts[d] = src.at[..., a, :], dst.at[..., b, :]
        return parts

    def merge(land, k, ref, phases, lo, hi):
        for p in range(phases):
            left = land[0, k, p, lo:hi]
            ref[2 * phases + p, lo:hi] = jnp.where(lanes_of(left) < HALF, land[1, k, p, lo:hi], left)

    def prepare(t):
        cols = slice(t * LANES, (t + 1) * LANES)
        active = vin[:, cols].astype(jnp.float32) * fin[0, t].astype(jnp.float32)
        nat[0, t, H0:H0 + N0] = active * gin[:, cols]
        nat[1, t, H0:H0 + N0] = active * OMEGA / (4.0 + win[:, cols])

    flag_copy.wait()
    for copy in loads[0] + loads[1]:
        copy.wait()
    for t in outer:
        prepare(t)
    own = slice(H0, H0 + N0)
    for side, near, far in ((0, 0, 1), (1, OWN - 1, OWN - 2)):
        for k in range(2):
            pack0[side, k, own] = group_phases(nat[k, near, own], near % 4)
        source, weight = group_phases(nat[0, far, own], far % 4), group_phases(nat[1, far, own], far % 4)
        low = (lanes_of(source) & 16) == 0
        if side == 0:
            pack0[side, 2, own] = jnp.where(low, source, pltpu.roll(weight, 16, 1))
        else:
            pack0[side, 2, own] = jnp.where(low, pltpu.roll(weight, LANES - 16, 1), source)
    interior = jnp.logical_and(lat > 0, lat < lat_count - 1).astype(jnp.int32)
    pl.semaphore_wait(barrier, 5 + 3 * interior)
    send(side_message)
    send(late_message)
    for copy in loads[2]:
        copy.wait()
    for t in inner:
        prepare(t)
    send(near_message)
    send(far_message)

    def arrange(t, lo, hi, arrays=(0, 1)):
        for k in arrays:
            ref = (s0, b0)[k]

            def store(p, part, x, ref=ref):
                ref[P0 * t + p, lo + O0 - H0 + part.start:lo + O0 - H0 + part.stop] = x

            def tile(j, part):
                if t < 2:
                    return mid[k, j, part]
                rows = slice(lo + part.start, lo + part.stop)
                side = 0 if j < 2 else 1
                if j in (0, 3):
                    return land0[side, k, rows]
                x = land0[side, 2, rows]
                if k == 1:
                    x = pltpu.roll(x, LANES - 16 if side == 0 else 16, 1)
                low = (lanes_of(x) & 16) == 0
                return jnp.where(low, x, 0.0) if side == 0 else jnp.where(low, 0.0, x)

            if t < 2:
                for j in range(4):
                    mid[k, j, 0:hi - lo] = group_phases(nat[k, 4 * t + j, lo:hi], j)
            split_phases([functools.partial(tile, j) for j in range(4)], hi - lo, store)

    def columns(t):
        return slice(t * LANES, (t + 1) * LANES)

    for t in range(2):
        arrange(t, H0, H0 + N0, (1,))

        def store_weight(p, part, x):
            w0[P0 * t + p, part.start + O0:part.stop + O0] = x

        for j in range(4):
            mid[0, j, 0:N0] = group_phases(win[:, columns(4 * t + j)], j)
        split_phases([lambda part, j=j: mid[0, j, part] for j in range(4)], N0, store_weight)
    own = slice(O0, O0 + N0)
    for i in range(2 * P0):
        v0[i, own] = jnp.where(b0[i, own] > 0.0, 1.0, 0.0)

    own = slice(O1, O1 + N1)
    for i in range(2 * P1):
        active = coarsen(v0, i, O0, N1, jnp.maximum)
        weight = coarsen(w0, i, O0, N1, jnp.add)
        diag = 4.0 + weight
        b1[i, own] = active * OMEGA / diag
        e1[i, own] = active * diag
        v1[i, own] = active
        u1[i, own] = weight
    message1 = (2, coarse_parts(bb, xbb, P1, O1, N1, H1))
    send(message1)

    for i in range(2 * P2):
        w2[i, O2:O2 + N2] = coarsen(u1, i, O1, N2, jnp.add)
        a2[i, O2:O2 + N2] = coarsen(v1, i, O1, N2, jnp.maximum)
    message2 = (3, coarse_parts(wa, xwa, P2, O2, N2, H2))
    send(message2)

    own = slice(O0, O0 + N0)
    for t in range(2):
        arrange(t, H0, H0 + N0, (0,))
    for i in range(2 * P0):
        e0[i, own] = jnp.where(b0[i, own] > 0.0, 4.0 + w0[i, own], 0.0)

    clear((nat.at[0], nat.at[1], land0.at[0], land0.at[1]), (0, H0), (H0 + N0, 2 * H0 + N0))

    def inverse(t, lo, hi):
        for i in range(P0 * t, P0 * t + P0):
            e0[i, lo + 8:hi + 8] = masked_inverse(b0[i, lo + 8:hi + 8])

    received(near_message)
    for t in range(T0 - 1):
        for lo, hi in ((8, H0), (H0 + N0, H0 + N0 + 8)):
            arrange(t, lo, hi)
            inverse(t, lo, hi)

    own = range(2 * P0)
    sides = range(2 * P0, n0)
    before, after = {0: (1, 2, 3), 1: (0, 1, 2)}, {0: (0,), 1: (3,), 2: (0, 1, 2, 3)}
    first_sweep(w0, s0, b0, own, *B0)
    sweep(w0, v0, s0, b0, P0, T0, *B0, before)

    middle, end = H0 + N0 // 2, 2 * H0 + N0
    received(side_message)
    arrange(T0 - 1, 0, middle)
    inverse(T0 - 1, 0, middle)
    received(late_message)
    arrange(T0 - 1, middle, end)
    inverse(T0 - 1, middle, end)
    first_sweep(w0, s0, b0, sides, *B0)
    sweep(w0, v0, s0, b0, P0, T0, *B0, after)
    column_residual(v0, s0, e0, P0, T0, *B0, tmp)

    for cycle in range(2):
        rows0 = A0 if cycle == 0 else B0
        g2 = gg.at[cycle]
        if cycle == 1:
            sweep(v0, w0, s0, b0, P0, T0, *B0)
            sweep(w0, v0, s0, b0, P0, T0, *B0)
            column_residual(v0, s0, e0, P0, T0, *B0, tmp)

        if cycle == 0:
            received(message1)
            clear((bb.at[0], xbb.at[0, 0], xbb.at[1, 0]), (O1 - H1, O1), (O1 + N1, O1 + N1 + H1))
            merge(xbb, 0, b1, P1, *A1)
            for i in range(2 * P1, n1):
                e1[i, O1:O1 + N1] = masked_inverse(b1[i, O1:O1 + N1])
        restrict(tmp, n1, A0[0], g1, b1, A1[0], A1[1] - A1[0])
        first_sweep(u1, g1, b1, range(n1), *A1)
        sweep(u1, v1, g1, b1, P1, T1, *A1)
        column_residual(v1, g1, e1, P1, T1, O1, O1 + N1, tmp)
        for t in range(n2):
            on = coarsen(b1, t, O1, N2, jnp.maximum) > 0.0
            g2[t, O2:O2 + N2] = jnp.where(on, rows_op(tmp, t, O1, N2, jnp.add), 0.0)
        message_g = (4 + cycle, row_parts(g2, g2, O2, N2, H2))
        message_v = (6 + cycle, row_parts(vg, rvg.at[cycle], O1, N1, H1))
        send(message_g)
        send(message_v)

        if cycle == 0:
            received(far_message)
            for lo, hi in ((0, 8), (H0 + N0 + 8, 2 * H0 + N0)):
                for t in range(T0 - 1):
                    arrange(t, lo, hi)
                first_sweep(w0, s0, b0, range(n0), lo + 8, hi + 8)
            for lo, hi in ((A0[0], A0[0] + 16), (A0[1] - 16, A0[1])):
                sweep(w0, v0, s0, b0, P0, T0, lo, hi)
            received(message2)
            clear((w2, a2, xwa.at[0, 0], xwa.at[0, 1], xwa.at[1, 0], xwa.at[1, 1]),
                  (O2 - H2, O2), (O2 + N2, O2 + N2 + H2))
            for k in range(2):
                merge(xwa, k, wa.at[k], P2, *A2)
            lo, hi = A2
            for t in range(n2):
                diag = 4.0 + w2[t, lo:hi]
                b2[t, lo:hi] = a2[t, lo:hi] * OMEGA / diag
                e2[t, lo:hi] = a2[t, lo:hi] * diag
            lo, hi = A3
            for t in range(n3):
                b3[t, lo:hi] = pack(a2, t, A2[0], hi - lo, jnp.maximum) * OMEGA / (
                    4.0 + pack(w2, t, A2[0], hi - lo, jnp.add))
        received(message_g)
        clear((g2,), (O2 - H2, O2), (O2 + N2, O2 + N2 + H2))
        first_sweep(u2, g2, b2, range(n2), *A2)
        sweep(u2, v2, g2, b2, P2, T2, *A2)
        for t in range(n2):
            r2[t, A2[0]:A2[1]] = residual_of(v2, g2, e2, t, P2, T2, *A2, (0,))[0]
        lo, hi = A3
        for t in range(n3):
            g3[t, lo:hi] = jnp.where(b3[t, lo:hi] > 0.0, pack(r2, t, A2[0], hi - lo, jnp.add), 0.0)
        first_sweep(v3, g3, b3, range(n3), *A3)
        for i in range(7):
            src, dst = (v3, u3) if i % 2 == 0 else (u3, v3)
            sweep(src, dst, g3, b3, P3, T3, *A3)
        unpack(u3, v2, b2, A3[0] + (B2[0] - A2[0]) // 2, (B2[1] - B2[0]) // 2, B2[0], tmp)
        sweep(v2, u2, g2, b2, P2, T2, *B2)
        sweep(u2, v2, g2, b2, P2, T2, *B2)

        sent(message_g)
        sent(message_v)
        received(message_v)
        clear((rvg.at[cycle, 0], rvg.at[cycle, 1]), (O1 - H1, O1), (O1 + N1, O1 + N1 + H1))
        for k in range(2):
            for i in range(n1):
                for lo, hi in ((A1[0], O1), (O1 + N1, A1[1])):
                    vg[k, i, lo:hi] = rvg[cycle, k, i, lo:hi]
        correct(v2, v1, b1, n2, O2 - 4, (A1[1] - A1[0]) // 2, A1[0], tmp)
        sweep(v1, u1, g1, b1, P1, T1, *A1)
        sweep(u1, v1, g1, b1, P1, T1, *A1)
        correct(v1, v0, b0, n1, A1[0], A1[1] - A1[0], A0[0], tmp)
        sweep(v0, w0, s0, b0, P0, T0, *rows0)
        sweep(w0, v0, s0, b0, P0, T0, *rows0)

    own = slice(O0, O0 + N0)
    for t in range(2):
        for p, r in enumerate(residual_of(v0, s0, e0, t, P0, T0, own.start, own.stop, tuple(range(P0)))):
            i = P0 * t + p
            out[i] = v0[i, own]
            res[i] = r
    for message in (side_message, late_message, near_message, far_message, message1, message2):
        sent(message)


def store(a, b, out, res, stage, mid, sem):
    copies = []
    for k, (src, dst) in enumerate(((a, out), (b, res))):
        for t in range(2):
            def store_tile(j, x):
                stage[k, :, (4 * t + j) * LANES:(4 * t + j + 1) * LANES] = x

            join_phases([lambda part, p=p: src[P0 * t + p, part] for p in range(P0)], mid, N0,
                        [functools.partial(store_tile, j) for j in range(4)])
            half = pl.ds(4 * t * LANES, 4 * LANES)
            copies.append(pltpu.make_async_copy(stage.at[k, :, half], dst.at[:, half], sem.at[k, t]))
            copies[-1].start()
    for copy in copies:
        copy.wait()


def solution(mesh):
    def body(guide, screen, valid, tiles):
        def vmem(*shape):
            return pltpu.VMEM(shape + (LANES,), jnp.float32)

        n0, n1, n2, n3 = P0 * T0, P1 * T1, P2 * T2, P3 * T3
        block = guide.shape
        guide, screen, valid, tiles = [
            pltpu.with_memory_space_constraint(x, pltpu.HBM) for x in (guide, screen, valid, tiles)]
        pair = pl.pallas_call(
            functools.partial(kernel, mesh.shape["lon"], mesh.shape["lat"]),
            out_shape=(pltpu.VMEM((2 * P0, N0, LANES), jnp.float32),) * 2,
            in_specs=[pl.BlockSpec(memory_space=pl.ANY)] * 4,
            out_specs=(pl.BlockSpec(memory_space=pltpu.VMEM),) * 2,
            scratch_shapes=[
                pltpu.VMEM(block, jnp.float32), pltpu.VMEM(block, jnp.float32), pltpu.VMEM(block, jnp.int32),
                pltpu.SMEM((1, OWN), jnp.int32),
                vmem(2, OWN, N0 + 2 * H0), vmem(2, 3, N0 + 2 * H0), vmem(2, 3, N0 + 2 * H0), vmem(2, 4, N0 + 2 * H0), vmem(n0, R0), vmem(n0, R0), vmem(n0, R0), vmem(n0, R0), vmem(n0, R0),
                vmem(n1, R0),
                vmem(2, n1, R1), vmem(1, n1, R1), vmem(n1, R1), vmem(n1, R1),
                vmem(2, n2, R2), vmem(n2, R2), vmem(n2, R2), vmem(2, n2, R2), vmem(n2, R2), vmem(n2, R2), vmem(n2, R2),
                vmem(n3, R3), vmem(n3, R3), vmem(n3, R3), vmem(n3, R3),
                vmem(2, 1, P1, R1), vmem(2, 2, P2, R2), vmem(2, 2, n1, R1),
                pltpu.SemaphoreType.DMA((4, 3)), pltpu.SemaphoreType.DMA((9, 8)),
                pltpu.SemaphoreType.DMA((9, 8)),
            ],
            compiler_params=pltpu.CompilerParams(
                collective_id=0, has_side_effects=True, vmem_limit_bytes=48 * 1024 * 1024),
        )(guide, screen, valid, tiles)
        pair = [pltpu.with_memory_space_constraint(x, pltpu.VMEM) for x in pair]
        return pl.pallas_call(
            store,
            out_shape=(pltpu.HBM(block, jnp.float32),) * 2,
            in_specs=[pl.BlockSpec(memory_space=pltpu.VMEM)] * 2,
            out_specs=(pl.BlockSpec(memory_space=pltpu.HBM),) * 2,
            scratch_shapes=[pltpu.VMEM((2,) + block, jnp.float32), vmem(4, N0), pltpu.SemaphoreType.DMA((2, 2))],
        )(*pair)

    spec = P("lat", "lon")
    return jax.shard_map(
        body, mesh=mesh, in_specs=(spec,) * 4, out_specs=(spec,) * 2, check_vma=False)
```

```python
import functools

import jax
import jax.numpy as jnp
from jax import lax
from jax.experimental import pallas as pl
from jax.experimental.pallas import tpu as pltpu
from jax.sharding import PartitionSpec as P

OMEGA = 0.8
MESH = pl.DeviceIdType.MESH
LANES = 128
CHUNK = 24
HALF = LANES // 2

P0, P1, P2, P3 = 4, 2, 1, 1
T0, T1, T2, T3 = 3, 3, 3, 2
O0, O1, O2, O3 = 24, 16, 32, 20
N0, N1, N2, N3 = 128, 64, 32, 16
R0, R1, R2, R3 = 176, 96, 96, 56
A0, B0, A1, A2, B2, A3 = (8, 168), (16, 160), (8, 88), (8, 88), (24, 72), (8, 48)
H0, H1, H2 = 16, 8, 24
OWN = 8
DIRS = ((-1, 0), (1, 0), (0, -1), (0, 1), (-1, -1), (-1, 1), (1, -1), (1, 1))


def lanes_of(x):
    return lax.broadcasted_iota(jnp.int32, x.shape, 1)


def gather(x, index):
    return jnp.take_along_axis(x, index, axis=1, mode="promise_in_bounds")


def barrel(tiles, lane):
    odd, high = (lane & 32) != 0, lane >= HALF
    half = [jnp.where(odd, tiles[(i + 1) % 4], tiles[i]) for i in range(4)]
    return [jnp.where(high, half[(i + 2) % 4], half[i]) for i in range(4)]


def group_phases(x, t):
    lane = lanes_of(x)
    return gather(x, ((lane & 31) << 2) + (((lane >> 5) + (4 - t)) & 3))


def split_phases(sources, rows, store):
    step = min(rows, 16)
    for row in range(0, rows, step):
        part = slice(row, row + step)
        tiles = [src(part) for src in sources]
        mixed = barrel(tiles, lanes_of(tiles[0]))
        store(0, part, mixed[0])
        for p in range(1, 4):
            store(p, part, pltpu.roll(mixed[4 - p], LANES - 32 * p, 1))


def join_phases(sources, mid, rows, stores):
    for row in range(0, rows, 16):
        part = slice(row, row + 16)
        phases = [src(part) for src in sources]
        placed = [phases[0]] + [pltpu.roll(phases[p], 32 * p, 1) for p in range(1, 4)]
        mixed = barrel(placed, lanes_of(placed[0]))
        for t in range(4):
            mid[t, part] = mixed[(4 - t) % 4]
    for t, store in enumerate(stores):
        x = mid[t, 0:rows]
        lane = lanes_of(x)
        store(gather(x, (((lane + t) & 3) << 5) + (lane >> 2)))


def neighbours(src, g, t, phases, count, lo, hi, wanted):
    base, last = t * phases, phases - 1
    row = [src[base + p, lo:hi] for p in range(phases)]
    lane = lanes_of(row[0])
    left = right = None
    if 0 in wanted:
        left = pltpu.roll(jnp.where(lane == LANES - 1, src[((t - 1) % count) * phases + last, lo:hi], row[last]), 1, 1)
    if last in wanted:
        right = pltpu.roll(jnp.where(lane == 0, src[((t + 1) % count) * phases, lo:hi], row[0]), LANES - 1, 1)
    row = [left] + row + [right]
    return [(p, row[p + 1], (g[base + p, lo:hi] + (src[base + p, lo - 1:hi - 1] + src[base + p, lo + 1:hi + 1])) + (
        row[p] + row[p + 2])) for p in wanted]


def everything(phases, count):
    return {t: tuple(range(phases)) for t in range(count)}


def sweep(src, dst, g, b, phases, count, lo, hi, wanted=None):
    wanted = wanted or everything(phases, count)
    for start in range(lo, hi, CHUNK):
        part = slice(start, min(start + CHUNK, hi))
        for t in wanted:
            for p, x, near in neighbours(src, g, t, phases, count, part.start, part.stop, wanted[t]):
                i = t * phases + p
                dst[i, part] = (1.0 - OMEGA) * x + b[i, part] * near


def first_sweep(dst, g, b, planes, lo, hi):
    for i in planes:
        dst[i, lo:hi] = b[i, lo:hi] * g[i, lo:hi]


def residual_of(src, g, e, t, phases, count, lo, hi, wanted):
    found = []
    for p, x, near in neighbours(src, g, t, phases, count, lo, hi, wanted):
        i = t * phases + p
        ee = e[i, lo:hi]
        found.append(jnp.where(ee > 0.0, near - ee * x, 0.0))
    return found


def column_residual(src, g, e, phases, count, lo, hi, tmp):
    wanted = everything(phases, count)
    for start in range(lo, hi, CHUNK):
        part = slice(start, min(start + CHUNK, hi))
        for t in wanted:
            r = residual_of(src, g, e, t, phases, count, part.start, part.stop, wanted[t])
            for k, p in enumerate(wanted[t][::2]):
                tmp[(t * phases + p) // 2, part] = r[2 * k] + r[2 * k + 1]


def rows_op(src, i, lo, rows, op):
    return op(src[i, pl.ds(lo, rows, stride=2)], src[i, pl.ds(lo + 1, rows, stride=2)])


def restrict(tmp, planes, tlo, out, active, olo, rows):
    for i in range(planes):
        out[i, olo:olo + rows] = jnp.where(
            active[i, olo:olo + rows] > 0.0, rows_op(tmp, i, tlo, rows, jnp.add), 0.0)


def coarsen(src, i, lo, rows, op):
    return op(rows_op(src, 2 * i, lo, rows, op), rows_op(src, 2 * i + 1, lo, rows, op))


def correct(coarse, fine, b, planes, clo, rows, lo, tmp):
    hi = lo + 2 * rows
    for i in range(planes):
        c = coarse[i, clo:clo + rows]
        tmp[i, pl.ds(lo, rows, stride=2)] = c
        tmp[i, pl.ds(lo + 1, rows, stride=2)] = c
    for i in range(2 * planes):
        fine[i, lo:hi] = fine[i, lo:hi] + jnp.where(b[i, lo:hi] > 0.0, tmp[i // 2, lo:hi], 0.0)


def pack(src, t, lo, rows, op):
    x = rows_op(src, 2 * t, lo, rows, op)
    lane = lanes_of(x)
    x = op(x, pltpu.roll(x, LANES - 1, 1))
    if 2 * t + 1 < T2:
        y = rows_op(src, 2 * t + 1, lo, rows, op)
        x = jnp.where((lane & 1) == 0, x, op(y, pltpu.roll(y, 1, 1)))
        index = jnp.where(lane < HALF, 2 * lane, 2 * lane - (LANES - 1))
    else:
        index = (2 * lane) & (LANES - 1)
    return gather(x, index)


def unpack(coarse, fine, b, clo, rows, lo, tmp):
    hi = lo + 2 * rows
    for t in range(T2):
        c = coarse[t // 2, clo:clo + rows]
        lane = lanes_of(c)
        if t == T2 - 1:
            index = (lane >> 1) + jnp.where(lane < HALF, 0, HALF)
        else:
            index = (lane >> 1) + HALF * (t % 2)
        c = gather(c, index)
        tmp[t, pl.ds(lo, rows, stride=2)] = c
        tmp[t, pl.ds(lo + 1, rows, stride=2)] = c
    for t in range(T2):
        fine[t, lo:hi] = fine[t, lo:hi] + jnp.where(b[t, lo:hi] > 0.0, tmp[t, lo:hi], 0.0)


def masked_inverse(x):
    return jnp.where(x > 0.0, OMEGA / jnp.where(x > 0.0, x, 1.0), 0.0)


def kernel(lon_count, lat_count, guide, screen, valid, tiles, out, res,
           gin, win, vin, fin, nat, pack0, land0, mid, s0, b0, e0, v0, w0, tmp, vg, bb, e1, u1, wa, b2, e2, gg, v2, u2, r2, b3, g3, v3, u3,
           xbb, xwa, rvg, in_sem, send_sem, recv_sem):
    lon = lax.axis_index("lon")
    lat = lax.axis_index("lat")
    v1, g1, b1 = vg.at[0], vg.at[1], bb.at[0]
    w2, a2 = wa.at[0], wa.at[1]
    n0, n1, n2, n3 = P0 * T0, P1 * T1, P2 * T2, P3 * T3

    def peer(d):
        return {"lat": lax.rem(lat + DIRS[d][0] + lat_count, lat_count),
                "lon": lax.rem(lon + DIRS[d][1] + lon_count, lon_count)}

    def exists(dy):
        return lat > 0 if dy < 0 else lat < lat_count - 1 if dy > 0 else None

    def guarded(condition, fn):
        if condition is None:
            fn()
        else:
            pl.when(condition)(fn)

    barrier = pltpu.get_barrier_semaphore()
    def by_row(directions, fn, sign=1):
        for dy in (-1, 1, 0):
            chosen = [d for d in directions if DIRS[d][0] == dy]

            def run(chosen=chosen):
                for d in chosen:
                    fn(d)

            if chosen:
                guarded(exists(sign * dy), run)

    by_row(range(8), lambda d: pl.semaphore_signal(barrier, inc=1, device_id=peer(d), device_id_type=MESH))

    outer, inner = (0, 1, OWN - 2, OWN - 1), tuple(range(2, OWN - 2))
    flag_copy = pltpu.make_async_copy(tiles, fin, in_sem.at[3, 0])
    loads = [[pltpu.make_async_copy(src.at[:, cols], dst.at[:, cols], in_sem.at[i, k])
              for i, (src, dst) in enumerate(((valid, vin), (screen, win), (guide, gin)))]
             for k, cols in enumerate((pl.ds(0, 2 * LANES), pl.ds((OWN - 2) * LANES, 2 * LANES),
                                       pl.ds(2 * LANES, (OWN - 4) * LANES)))]
    flag_copy.start()
    for part in loads:
        for copy in part:
            copy.start()

    for ref, lo, hi in ((v0, *A0), (w0, *A0), (v1, *A1), (u1, *A1), (v2, *A2), (u2, *A2), (v3, *A3), (u3, *A3)):
        zero = jnp.zeros((ref.shape[0], 8, LANES), jnp.float32)
        ref[:, lo - 8:lo] = zero
        ref[:, hi:hi + 8] = zero

    def copy_of(message, d):
        kind, parts = message
        src, dst = parts[d]
        return pltpu.make_async_remote_copy(
            src_ref=src, dst_ref=dst, send_sem=send_sem.at[kind, d], recv_sem=recv_sem.at[kind, d],
            device_id=peer(d), device_id_type=MESH)

    def send(message):
        by_row(message[1], lambda d: copy_of(message, d).start())

    def sent(message):
        by_row(message[1], lambda d: copy_of(message, d).wait_send())

    def received(message):
        by_row(message[1], lambda d: copy_of(message, d).wait_recv(), -1)

    def clear(refs, above, below):
        for edge, rows in ((lat == 0, above), (lat == lat_count - 1, below)):
            @pl.when(edge)
            def _():
                for ref in refs:
                    zero = jnp.zeros((rows[1] - rows[0], LANES), jnp.float32)
                    for i in range(ref.shape[0]):
                        ref[i, rows[0]:rows[1]] = zero

    def row_spans(dy, first, rows, depth, skip=0):
        if dy < 0:
            return pl.ds(first + skip, depth), pl.ds(first + rows + skip, depth)
        if dy > 0:
            return pl.ds(first + rows - depth - skip, depth), pl.ds(first - depth - skip, depth)
        return (pl.ds(first, rows),) * 2

    near_parts, far_parts, side_parts, late_parts = {}, {}, {}, {}
    for d, (dy, dx) in enumerate(DIRS):
        if dx == 0:
            for parts, skip in ((near_parts, 0), (far_parts, 8)):
                a, b = row_spans(dy, H0, N0, 8, skip)
                parts[d] = nat.at[:, :, a], nat.at[:, :, b]
        else:
            a, b = row_spans(dy, H0, N0, H0)
            side = 0 if dx < 0 else 1
            if dy == 0:
                a, late = (pl.ds(H0 + k * (N0 // 2), N0 // 2) for k in range(2))
                b = a
                late_parts[d] = pack0.at[side, :, late], land0.at[side, :, late]
            side_parts[d] = pack0.at[side, :, a], land0.at[side, :, b]
    near_message, far_message = (0, near_parts), (1, far_parts)
    side_message, late_message = (0, side_parts), (8, late_parts)

    def coarse_parts(ref, land, phases, first, rows, depth):
        parts = {}
        for d, (dy, dx) in enumerate(DIRS):
            a, b = row_spans(dy, first, rows, depth)
            if dx == 0:
                own = pl.ds(0, 2 * phases)
                parts[d] = ref.at[:, own, a], ref.at[:, own, b]
            else:
                mine, side = (0, 1) if dx < 0 else (phases, 0)
                parts[d] = ref.at[:, pl.ds(mine, phases), a], land.at[side, :, :, b]
        return parts

    def row_parts(src, dst, first, rows, depth):
        parts = {}
        for d in range(2):
            a, b = row_spans(DIRS[d][0], first, rows, depth)
            parts[d] = src.at[..., a, :], dst.at[..., b, :]
        return parts

    def merge(land, k, ref, phases, lo, hi):
        for p in range(phases):
            left = land[0, k, p, lo:hi]
            ref[2 * phases + p, lo:hi] = jnp.where(lanes_of(left) < HALF, land[1, k, p, lo:hi], left)

    def prepare(t):
        cols = slice(t * LANES, (t + 1) * LANES)
        active = vin[:, cols].astype(jnp.float32) * fin[0, t].astype(jnp.float32)
        nat[0, t, H0:H0 + N0] = active * gin[:, cols]
        nat[1, t, H0:H0 + N0] = active * OMEGA / (4.0 + win[:, cols])

    flag_copy.wait()
    for copy in loads[0] + loads[1]:
        copy.wait()
    for t in outer:
        prepare(t)
    own = slice(H0, H0 + N0)
    for side, near, far in ((0, 0, 1), (1, OWN - 1, OWN - 2)):
        for k in range(2):
            pack0[side, k, own] = group_phases(nat[k, near, own], near % 4)
        source, weight = group_phases(nat[0, far, own], far % 4), group_phases(nat[1, far, own], far % 4)
        low = (lanes_of(source) & 16) == 0
        if side == 0:
            pack0[side, 2, own] = jnp.where(low, source, pltpu.roll(weight, 16, 1))
        else:
            pack0[side, 2, own] = jnp.where(low, pltpu.roll(weight, LANES - 16, 1), source)
    interior = jnp.logical_and(lat > 0, lat < lat_count - 1).astype(jnp.int32)
    pl.semaphore_wait(barrier, 5 + 3 * interior)
    send(side_message)
    send(late_message)
    for copy in loads[2]:
        copy.wait()
    for t in inner:
        prepare(t)
    send(near_message)
    send(far_message)

    def arrange(t, lo, hi, arrays=(0, 1)):
        for k in arrays:
            ref = (s0, b0)[k]

            def store(p, part, x, ref=ref):
                ref[P0 * t + p, lo + O0 - H0 + part.start:lo + O0 - H0 + part.stop] = x

            def tile(j, part):
                if t < 2:
                    return mid[k, j, part]
                rows = slice(lo + part.start, lo + part.stop)
                side = 0 if j < 2 else 1
                if j in (0, 3):
                    return land0[side, k, rows]
                x = land0[side, 2, rows]
                if k == 1:
                    x = pltpu.roll(x, LANES - 16 if side == 0 else 16, 1)
                low = (lanes_of(x) & 16) == 0
                return jnp.where(low, x, 0.0) if side == 0 else jnp.where(low, 0.0, x)

            if t < 2:
                for j in range(4):
                    mid[k, j, 0:hi - lo] = group_phases(nat[k, 4 * t + j, lo:hi], j)
            split_phases([functools.partial(tile, j) for j in range(4)], hi - lo, store)

    def columns(t):
        return slice(t * LANES, (t + 1) * LANES)

    for t in range(2):
        arrange(t, H0, H0 + N0, (1,))

        def store_weight(p, part, x):
            w0[P0 * t + p, part.start + O0:part.stop + O0] = x

        for j in range(4):
            mid[0, j, 0:N0] = group_phases(win[:, columns(4 * t + j)], j)
        split_phases([lambda part, j=j: mid[0, j, part] for j in range(4)], N0, store_weight)
    own = slice(O0, O0 + N0)
    for i in range(2 * P0):
        v0[i, own] = jnp.where(b0[i, own] > 0.0, 1.0, 0.0)

    own = slice(O1, O1 + N1)
    for i in range(2 * P1):
        active = coarsen(v0, i, O0, N1, jnp.maximum)
        weight = coarsen(w0, i, O0, N1, jnp.add)
        diag = 4.0 + weight
        b1[i, own] = active * OMEGA / diag
        e1[i, own] = active * diag
        v1[i, own] = active
        u1[i, own] = weight
    message1 = (2, coarse_parts(bb, xbb, P1, O1, N1, H1))
    send(message1)

    for i in range(2 * P2):
        w2[i, O2:O2 + N2] = coarsen(u1, i, O1, N2, jnp.add)
        a2[i, O2:O2 + N2] = coarsen(v1, i, O1, N2, jnp.maximum)
    message2 = (3, coarse_parts(wa, xwa, P2, O2, N2, H2))
    send(message2)

    own = slice(O0, O0 + N0)
    for t in range(2):
        arrange(t, H0, H0 + N0, (0,))
    for i in range(2 * P0):
        e0[i, own] = jnp.where(b0[i, own] > 0.0, 4.0 + w0[i, own], 0.0)

    clear((nat.at[0], nat.at[1], land0.at[0], land0.at[1]), (0, H0), (H0 + N0, 2 * H0 + N0))

    def inverse(t, lo, hi):
        for i in range(P0 * t, P0 * t + P0):
            e0[i, lo + 8:hi + 8] = masked_inverse(b0[i, lo + 8:hi + 8])

    received(near_message)
    for t in range(T0 - 1):
        for lo, hi in ((8, H0), (H0 + N0, H0 + N0 + 8)):
            arrange(t, lo, hi)
            inverse(t, lo, hi)

    own = range(2 * P0)
    sides = range(2 * P0, n0)
    before, after = {0: (1, 2, 3), 1: (0, 1, 2)}, {0: (0,), 1: (3,), 2: (0, 1, 2, 3)}
    first_sweep(w0, s0, b0, own, *B0)
    sweep(w0, v0, s0, b0, P0, T0, *B0, before)

    middle, end = H0 + N0 // 2, 2 * H0 + N0
    received(side_message)
    arrange(T0 - 1, 0, middle)
    inverse(T0 - 1, 0, middle)
    lo, hi = B0
    ready = middle + 8
    first_sweep(w0, s0, b0, sides, lo, ready)
    sweep(w0, v0, s0, b0, P0, T0, lo, ready - 8, after)
    column_residual(v0, s0, e0, P0, T0, lo, ready - 16, tmp)
    received(late_message)
    arrange(T0 - 1, middle, end)
    inverse(T0 - 1, middle, end)
    first_sweep(w0, s0, b0, sides, ready, hi)
    sweep(w0, v0, s0, b0, P0, T0, ready - 8, hi, after)
    column_residual(v0, s0, e0, P0, T0, ready - 16, hi, tmp)

    for cycle in range(2):
        rows0 = A0 if cycle == 0 else B0
        g2 = gg.at[cycle]
        if cycle == 1:
            sweep(v0, w0, s0, b0, P0, T0, *B0)
            sweep(w0, v0, s0, b0, P0, T0, *B0)
            column_residual(v0, s0, e0, P0, T0, *B0, tmp)

        if cycle == 0:
            received(message1)
            clear((bb.at[0], xbb.at[0, 0], xbb.at[1, 0]), (O1 - H1, O1), (O1 + N1, O1 + N1 + H1))
            merge(xbb, 0, b1, P1, *A1)
            for i in range(2 * P1, n1):
                e1[i, O1:O1 + N1] = masked_inverse(b1[i, O1:O1 + N1])
        restrict(tmp, n1, A0[0], g1, b1, A1[0], A1[1] - A1[0])
        first_sweep(u1, g1, b1, range(n1), *A1)
        sweep(u1, v1, g1, b1, P1, T1, *A1)
        column_residual(v1, g1, e1, P1, T1, O1, O1 + N1, tmp)
        for t in range(n2):
            on = coarsen(b1, t, O1, N2, jnp.maximum) > 0.0
            g2[t, O2:O2 + N2] = jnp.where(on, rows_op(tmp, t, O1, N2, jnp.add), 0.0)
        message_g = (4 + cycle, row_parts(g2, g2, O2, N2, H2))
        message_v = (6 + cycle, row_parts(vg, rvg.at[cycle], O1, N1, H1))
        send(message_g)
        send(message_v)

        if cycle == 0:
            received(far_message)
            for lo, hi in ((0, 8), (H0 + N0 + 8, 2 * H0 + N0)):
                for t in range(T0 - 1):
                    arrange(t, lo, hi)
                first_sweep(w0, s0, b0, range(n0), lo + 8, hi + 8)
            for lo, hi in ((A0[0], A0[0] + 16), (A0[1] - 16, A0[1])):
                sweep(w0, v0, s0, b0, P0, T0, lo, hi)
            received(message2)
            clear((w2, a2, xwa.at[0, 0], xwa.at[0, 1], xwa.at[1, 0], xwa.at[1, 1]),
                  (O2 - H2, O2), (O2 + N2, O2 + N2 + H2))
            for k in range(2):
                merge(xwa, k, wa.at[k], P2, *A2)
            lo, hi = A2
            for t in range(n2):
                diag = 4.0 + w2[t, lo:hi]
                b2[t, lo:hi] = a2[t, lo:hi] * OMEGA / diag
                e2[t, lo:hi] = a2[t, lo:hi] * diag
            lo, hi = A3
            for t in range(n3):
                b3[t, lo:hi] = pack(a2, t, A2[0], hi - lo, jnp.maximum) * OMEGA / (
                    4.0 + pack(w2, t, A2[0], hi - lo, jnp.add))
        received(message_g)
        clear((g2,), (O2 - H2, O2), (O2 + N2, O2 + N2 + H2))
        first_sweep(u2, g2, b2, range(n2), *A2)
        sweep(u2, v2, g2, b2, P2, T2, *A2)
        for t in range(n2):
            r2[t, A2[0]:A2[1]] = residual_of(v2, g2, e2, t, P2, T2, *A2, (0,))[0]
        lo, hi = A3
        for t in range(n3):
            g3[t, lo:hi] = jnp.where(b3[t, lo:hi] > 0.0, pack(r2, t, A2[0], hi - lo, jnp.add), 0.0)
        first_sweep(v3, g3, b3, range(n3), *A3)
        for i in range(7):
            src, dst = (v3, u3) if i % 2 == 0 else (u3, v3)
            sweep(src, dst, g3, b3, P3, T3, *A3)
        unpack(u3, v2, b2, A3[0] + (B2[0] - A2[0]) // 2, (B2[1] - B2[0]) // 2, B2[0], tmp)
        sweep(v2, u2, g2, b2, P2, T2, *B2)
        sweep(u2, v2, g2, b2, P2, T2, *B2)

        sent(message_g)
        sent(message_v)
        received(message_v)
        clear((rvg.at[cycle, 0], rvg.at[cycle, 1]), (O1 - H1, O1), (O1 + N1, O1 + N1 + H1))
        for k in range(2):
            for i in range(n1):
                for lo, hi in ((A1[0], O1), (O1 + N1, A1[1])):
                    vg[k, i, lo:hi] = rvg[cycle, k, i, lo:hi]
        correct(v2, v1, b1, n2, O2 - 4, (A1[1] - A1[0]) // 2, A1[0], tmp)
        sweep(v1, u1, g1, b1, P1, T1, *A1)
        sweep(u1, v1, g1, b1, P1, T1, *A1)
        correct(v1, v0, b0, n1, A1[0], A1[1] - A1[0], A0[0], tmp)
        sweep(v0, w0, s0, b0, P0, T0, *rows0)
        sweep(w0, v0, s0, b0, P0, T0, *rows0)

    own = slice(O0, O0 + N0)
    for t in range(2):
        for p, r in enumerate(residual_of(v0, s0, e0, t, P0, T0, own.start, own.stop, tuple(range(P0)))):
            i = P0 * t + p
            out[i] = v0[i, own]
            res[i] = r
    for message in (side_message, late_message, near_message, far_message, message1, message2):
        sent(message)


def store(a, b, out, res, stage, mid, sem):
    copies = []
    for k, (src, dst) in enumerate(((a, out), (b, res))):
        for t in range(2):
            def store_tile(j, x):
                stage[k, :, (4 * t + j) * LANES:(4 * t + j + 1) * LANES] = x

            join_phases([lambda part, p=p: src[P0 * t + p, part] for p in range(P0)], mid, N0,
                        [functools.partial(store_tile, j) for j in range(4)])
            half = pl.ds(4 * t * LANES, 4 * LANES)
            copies.append(pltpu.make_async_copy(stage.at[k, :, half], dst.at[:, half], sem.at[k, t]))
            copies[-1].start()
    for copy in copies:
        copy.wait()


def solution(mesh):
    def body(guide, screen, valid, tiles):
        def vmem(*shape):
            return pltpu.VMEM(shape + (LANES,), jnp.float32)

        n0, n1, n2, n3 = P0 * T0, P1 * T1, P2 * T2, P3 * T3
        block = guide.shape
        guide, screen, valid, tiles = [
            pltpu.with_memory_space_constraint(x, pltpu.HBM) for x in (guide, screen, valid, tiles)]
        pair = pl.pallas_call(
            functools.partial(kernel, mesh.shape["lon"], mesh.shape["lat"]),
            out_shape=(pltpu.VMEM((2 * P0, N0, LANES), jnp.float32),) * 2,
            in_specs=[pl.BlockSpec(memory_space=pl.ANY)] * 4,
            out_specs=(pl.BlockSpec(memory_space=pltpu.VMEM),) * 2,
            scratch_shapes=[
                pltpu.VMEM(block, jnp.float32), pltpu.VMEM(block, jnp.float32), pltpu.VMEM(block, jnp.int32),
                pltpu.SMEM((1, OWN), jnp.int32),
                vmem(2, OWN, N0 + 2 * H0), vmem(2, 3, N0 + 2 * H0), vmem(2, 3, N0 + 2 * H0), vmem(2, 4, N0 + 2 * H0), vmem(n0, R0), vmem(n0, R0), vmem(n0, R0), vmem(n0, R0), vmem(n0, R0),
                vmem(n1, R0),
                vmem(2, n1, R1), vmem(1, n1, R1), vmem(n1, R1), vmem(n1, R1),
                vmem(2, n2, R2), vmem(n2, R2), vmem(n2, R2), vmem(2, n2, R2), vmem(n2, R2), vmem(n2, R2), vmem(n2, R2),
                vmem(n3, R3), vmem(n3, R3), vmem(n3, R3), vmem(n3, R3),
                vmem(2, 1, P1, R1), vmem(2, 2, P2, R2), vmem(2, 2, n1, R1),
                pltpu.SemaphoreType.DMA((4, 3)), pltpu.SemaphoreType.DMA((9, 8)),
                pltpu.SemaphoreType.DMA((9, 8)),
            ],
            compiler_params=pltpu.CompilerParams(
                collective_id=0, has_side_effects=True, vmem_limit_bytes=48 * 1024 * 1024),
        )(guide, screen, valid, tiles)
        pair = [pltpu.with_memory_space_constraint(x, pltpu.VMEM) for x in pair]
        return pl.pallas_call(
            store,
            out_shape=(pltpu.HBM(block, jnp.float32),) * 2,
            in_specs=[pl.BlockSpec(memory_space=pltpu.VMEM)] * 2,
            out_specs=(pl.BlockSpec(memory_space=pltpu.HBM),) * 2,
            scratch_shapes=[pltpu.VMEM((2,) + block, jnp.float32), vmem(4, N0), pltpu.SemaphoreType.DMA((2, 2))],
        )(*pair)

    spec = P("lat", "lon")
    return jax.shard_map(
        body, mesh=mesh, in_specs=(spec,) * 4, out_specs=(spec,) * 2, check_vma=False)
```
